512 devices in a mesh: tile: 64 (over z, y_lo, core), scan: 8 (over y_hi, x).
Axes of the slice: x: 4, y: 4 (y_hi: 2, y_lo: 2; y = y_hi * 2 + y_lo), z: 16, core: 2. Of those that a mesh axis runs over, the one named last changes fastest.
Arguments:
- object_slices: float32 [2, 4, 4096, 256], P(None, None, ('tile', 'scan')), may hold values from -1 to 1
- probe_wave: float32 [2, 128, 128], replicated, may hold values from -2.5 to 2.5
- offsets: int32 [1024, 2], P(('tile', 'scan')), may hold values from 0 to 128, as said below
- counts: int32 [512], P(('tile', 'scan')), may hold values from 0 to 2, as said below
- measured: float32 [1024, 128, 128], P(('tile', 'scan')), may hold values from 0.05 to 2
Outputs:
- updated_slices: float32 [2, 4, 4096, 256], P(None, None, ('tile', 'scan'))
The draws below stay inside these ranges and needn't reach their ends.
Inputs may be any that keep to these rules, and one draw needn't show every extreme that they name: Slot p's patch starts at row (t * 64 - 128 / 2 + offsets[p, 0]) mod 4096, t the tile index holding slot p, and at column offsets[p, 1]; offsets[p, 0] < 64 and offsets[p, 1] <= 128. The counts of the devices of one tile index sum to 8 and one of them is 2; a device's slots at or past its count hold no position.
All inputs are finite; a program needn't handle non-finite values.
Results may differ from the reference program's by a relative error of at most 0.0003.
Values sent between devices are 32-bit elements; how exact they have to be, the bound alone decides.
A program may use at most 64 MiB of HBM per device.

```python
import math
import jax
import jax.numpy as jnp
from jax import lax

S = 4
W = 128
BAND = 64
NC = 256
POS_CAP = 2
ITERS = 2
NR = 4096
POSITIONS = 1024
N_TILE = 64
N_SCAN = 8


def draw_object_slices(key, part):
    key = jax.random.fold_in(key, 11)
    key_amp, key_phase = jax.random.split(key)
    grid_shape = (S, NR, NC)
    amplitude = jax.random.uniform(key_amp, grid_shape, jnp.float32, 0.7, 1.0)
    phases = jax.random.uniform(key_phase, grid_shape, jnp.float32, -math.pi, math.pi)
    return jnp.stack([amplitude * jnp.cos(phases), amplitude * jnp.sin(phases)]).astype(jnp.float32)


def draw_probe_wave(key, part):
    key = jax.random.fold_in(key, 23)
    key_re, key_im = jax.random.split(key)
    centre = (W - 1) / 2.0
    coords = (jnp.arange(W, dtype=jnp.float32) - centre) / (W / 3.0)
    distance = coords[:, None] * coords[:, None] + coords[None, :] * coords[None, :]
    envelope = 0.5 + 0.5 * jnp.exp(-distance)
    part_re = envelope * 0.7 * jnp.clip(jax.random.normal(key_re, (W, W), jnp.float32), -3.5, 3.5)
    part_im = envelope * 0.7 * jnp.clip(jax.random.normal(key_im, (W, W), jnp.float32), -3.5, 3.5)
    return jnp.stack([part_re, part_im]).astype(jnp.float32)


def draw_offsets(key, part):
    key = jax.random.fold_in(key, 37)
    key_row, key_col = jax.random.split(key)
    slot_total = POS_CAP * N_TILE * N_SCAN
    row_part = jax.random.randint(key_row, (slot_total,), 0, BAND, dtype=jnp.int32)
    col_part = jax.random.randint(key_col, (slot_total,), 0, NC - W + 1, dtype=jnp.int32)
    row_part = row_part.at[0].set(0).at[1].set(BAND - 1)
    col_part = col_part.at[0].set(0).at[1].set(NC - W)
    return jnp.stack([row_part, col_part], axis=1).astype(jnp.int32)


def draw_counts(key, part):
    key = jax.random.fold_in(key, 53)
    key_full, key_drop = jax.random.split(key)
    half_cap = POS_CAP // 2
    full_member = jax.random.randint(key_full, (N_TILE,), 0, N_SCAN, dtype=jnp.int32)
    dropped = jax.random.randint(key_drop, (N_TILE, half_cap), 0, N_SCAN - 1, dtype=jnp.int32)
    dropped = dropped + (dropped >= full_member[:, None]).astype(jnp.int32)
    members = jnp.arange(N_SCAN, dtype=jnp.int32)
    removed = jnp.sum((dropped[:, :, None] == members[None, None, :]).astype(jnp.int32), axis=1)
    live_counts = jnp.where(members[None, :] == full_member[:, None], POS_CAP, half_cap - removed)
    return live_counts.reshape(N_TILE * N_SCAN).astype(jnp.int32)


def steps_of(rng, shape, cuts, least, high):
    gain = 1.0
    for axis_at, blocks in cuts:
        draws = jax.random.uniform(jax.random.fold_in(jax.random.fold_in(rng, 6), axis_at), (blocks,), jnp.float32, least / len(cuts), high / len(cuts))
        gain = gain * jnp.repeat(jnp.exp(draws), shape[axis_at] // blocks).reshape((-1,) + (1,) * (len(shape) - 1 - axis_at))
    return gain


def setup_inputs(seed: int = 0) -> dict:
    key_list = jax.random.split(jax.random.key(seed), 6)
    return {
        "object_slices": draw_object_slices(jax.random.fold_in(key_list[5], 71), 0),
        "probe_wave": draw_probe_wave(jax.random.fold_in(key_list[5], 71), 0),
        "offsets": draw_offsets(jax.random.fold_in(key_list[5], 71), 0),
        "counts": draw_counts(jax.random.fold_in(key_list[5], 71), 0),
        "measured": jnp.clip(jnp.exp(math.log(2.0) - 3.6888794 * jax.random.uniform(key_list[4], (POSITIONS, W, W), jnp.float32) ** steps_of(key_list[4], (POSITIONS, W, W), ((0, 512),), -0.2, 0.2)), 0.05, 2.0),
    }


floor_power = 0.04
step_gain = 0.5

def fresnel_kernel():
    indices = jnp.arange(W, dtype=jnp.int32)
    frequency = ((indices + W // 2) % W - W // 2).astype(jnp.float32)
    squares = frequency[:, None] * frequency[:, None] + frequency[None, :] * frequency[None, :]
    angles = -math.pi / (2.0 * W) * squares
    return lax.complex(jnp.cos(angles), jnp.sin(angles))

def propagate(field, transfer):
    return jnp.fft.ifft2(transfer * jnp.fft.fft2(field, norm='ortho'), norm='ortho')

def forward_back(patch_field, probe_field, measured_block, live_mask, kernel):
    wave = probe_field[None] * patch_field[:, 0]
    arrivals = [None] * S
    for slice_index in range(1, S):
        arrived = propagate(wave, kernel)
        arrivals[slice_index] = arrived
        wave = arrived * patch_field[:, slice_index]
    far_field = jnp.fft.fft2(wave, norm='ortho')
    intensity = jnp.real(far_field) * jnp.real(far_field) + jnp.imag(far_field) * jnp.imag(far_field)
    amp_ratio = measured_block * lax.rsqrt(jnp.maximum(intensity, floor_power))
    residual = live_mask[:, None, None] * (far_field - amp_ratio * far_field)
    backward = jnp.fft.ifft2(residual, norm='ortho')
    gradients = [None] * S
    for slice_index in range(S - 1, 0, -1):
        gradients[slice_index] = jnp.conj(arrivals[slice_index]) * backward
        backward = propagate(jnp.conj(patch_field[:, slice_index]) * backward, jnp.conj(kernel))
    gradients[0] = jnp.conj(probe_field)[None] * backward
    return jnp.stack(gradients, axis=1)

def reference(object_slices, probe_wave, offsets, counts, measured):
    half_side = W // 2
    probe_field = lax.complex(probe_wave[0], probe_wave[1])
    step_size = step_gain / (jnp.max(probe_wave[0] * probe_wave[0] + probe_wave[1] * probe_wave[1]) + 1e-06)
    kernel = fresnel_kernel()
    groups = N_TILE * N_SCAN
    offset_blocks = offsets.reshape(groups, POS_CAP, 2)
    measured_blocks = measured.reshape(groups, POS_CAP, W, W)
    tile_of_block = (jnp.arange(groups, dtype=jnp.int32) // N_SCAN).astype(jnp.int32)
    slot_index = jnp.arange(POS_CAP, dtype=jnp.int32)
    anchor = jnp.zeros((), jnp.int32)
    current = object_slices
    for iteration in range(ITERS):
        extended = jnp.concatenate([current[:, :, NR - half_side:], current, current[:, :, :half_side]], axis=2)

        def one_block(accumulated, inputs):
            offset_block, measured_block, live_count, tile_index = inputs
            row_starts = (tile_index * BAND + offset_block[:, 0]).astype(jnp.int32)
            col_starts = offset_block[:, 1].astype(jnp.int32)

            def cut(row_start, col_start):
                return lax.dynamic_slice(extended, (anchor, anchor, row_start, col_start), (2, S, W, W))
            patches = jax.vmap(cut)(row_starts, col_starts)
            live_mask = (slot_index < live_count).astype(jnp.float32)
            gradients = forward_back(lax.complex(patches[:, 0], patches[:, 1]), probe_field, measured_block, live_mask, kernel)
            grad_pairs = jnp.stack([jnp.real(gradients), jnp.imag(gradients)], axis=1)

            def add_one(position, total):
                corner = (anchor, anchor, row_starts[position], col_starts[position])
                current_patch = lax.dynamic_slice(total, corner, (2, S, W, W))
                return lax.dynamic_update_slice(total, current_patch + grad_pairs[position], corner)
            return (lax.fori_loop(0, POS_CAP, add_one, accumulated), None)
        start_total = jnp.zeros((2, S, NR + W, NC), jnp.float32)
        accumulated, unused = lax.scan(one_block, start_total, (offset_blocks, measured_blocks, counts, tile_of_block))
        gradient = accumulated[:, :, half_side:half_side + NR]
        gradient = gradient.at[:, :, NR - half_side:].add(accumulated[:, :, :half_side])
        gradient = gradient.at[:, :, :half_side].add(accumulated[:, :, NR + half_side:])
        current = current - step_size * gradient
    return current
```

```python
import functools

import jax
import jax.numpy as jnp
import ml_dtypes
import numpy as np
from jax import lax
from jax.experimental import pallas as pl
from jax.experimental.pallas import tpu as pltpu
from jax.sharding import PartitionSpec as P


ITERS = 2
S = 4
W = 128
SCAN = 8
ROWS = 8
PROP, PROP_C, DFT, DFT_C = range(4)
MESH = pl.DeviceIdType.MESH
F32 = jnp.float32
BF16 = jnp.bfloat16
VMEM_BYTES = 48 * 2**20


def tables():
    n = np.arange(W)
    dft = np.exp(-2j * np.pi * (n[:, None] * n[None, :] % W) / W) / np.sqrt(W)
    freq = (n + W // 2) % W - W // 2
    prop = np.conj(dft) @ (np.exp(-1j * np.pi * freq * freq / (2.0 * W))[:, None] * dft)
    lefts, rights = [], []
    for m in (prop, np.conj(prop), dft, np.conj(dft)):
        right = np.block([[m.real, m.imag], [-m.imag, m.real]])
        left = np.block([[m.real, -m.imag], [m.imag, m.real]])
        for big, out, axis in ((right, rights, 0), (left, lefts, 1)):
            high = big.astype(ml_dtypes.bfloat16)
            low = (big - high.astype(np.float64)).astype(ml_dtypes.bfloat16)
            out.append(np.concatenate([high, high, low], axis=axis))
    return np.stack(lefts), np.stack(rights)


def halves(value):
    high = value.astype(BF16)
    return high, (value - high.astype(F32)).astype(BF16)


def sandwich(re, im, left_ref, right_ref, which):
    high, low = halves(jnp.concatenate([re, im], axis=0))
    mid = jnp.dot(left_ref[which], jnp.concatenate([high, low, high], axis=0), preferred_element_type=F32)
    high, low = halves(jnp.concatenate([mid[:W], mid[W:]], axis=1))
    out = jnp.dot(jnp.concatenate([high, low, high], axis=1), right_ref[which], preferred_element_type=F32)
    return out[:, :W], out[:, W:]


def mul(a, b):
    return a[0] * b[0] - a[1] * b[1], a[0] * b[1] + a[1] * b[0]


def mul_conj(a, b):
    return a[0] * b[0] + a[1] * b[1], a[0] * b[1] - a[1] * b[0]


def shifted(value, amount, axis):
    for bit in range(7):
        moved = pltpu.roll(value, 1 << bit, axis)
        value = jnp.where(lax.rem(lax.div(amount, 1 << bit), 2) == 1, moved, value)
    return value


def kernel(
    tiles, offsets_ref, counts_ref, object_ref, probe_ref, measured_ref, lefts_ref, rights_ref, out_ref,
    obj, probe, shift_probe, meas, meas_in, left, right, meta_out, meta, jobs, patch, gather_out, grad, grad_in,
    part, cross_in, last_in, near_send, near_recv, meta_send, meta_recv, meas_send, meas_recv, gather_send,
    gather_recv, reduce_send, reduce_recv, cross_send, cross_recv, last_send, last_recv, local_sem,
):
    tile = lax.axis_index("tile")
    me = lax.axis_index("scan")
    group = [(tile, lax.rem(me + j, SCAN)) for j in range(SCAN)]
    source = [lax.rem(me + SCAN - j, SCAN) for j in range(SCAN)]
    around = {d: (lax.rem(tile + d + tiles, tiles), me) for d in (-2, -1, 1, 2)}
    my_rows = pl.ds(pl.multiple_of(me * ROWS, ROWS), ROWS)

    barrier = pltpu.get_barrier_semaphore()
    for device in group[1:] + list(around.values()):
        pl.semaphore_signal(barrier, inc=1, device_id=device, device_id_type=MESH)

    locals_ = [
        pltpu.make_async_copy(object_ref, obj.at[1], local_sem.at[0]),
        pltpu.make_async_copy(probe_ref, probe, local_sem.at[1]),
        pltpu.make_async_copy(measured_ref.at[0], meas, local_sem.at[2]),
        pltpu.make_async_copy(lefts_ref, left, local_sem.at[3]),
        pltpu.make_async_copy(rights_ref, right, local_sem.at[4]),
    ]
    for copy in locals_:
        copy.start()

    row = lax.broadcasted_iota(jnp.int32, (ROWS, W), 0)
    lane = lax.broadcasted_iota(jnp.int32, (ROWS, W), 1)
    fields = [counts_ref[0], offsets_ref[0, 0], offsets_ref[0, 1], offsets_ref[1, 0], offsets_ref[1, 1]]
    packed = jnp.zeros((ROWS, W), jnp.int32)
    for f, field in enumerate(fields):
        packed = jnp.where(row == f, field, packed)
    meta_out[...] = packed
    meta[me] = packed

    pl.semaphore_wait(barrier, SCAN - 1 + 4)

    def send(src, dst, send_sem, recv_sem, device):
        copy = pltpu.make_async_remote_copy(
            src_ref=src, dst_ref=dst, send_sem=send_sem, recv_sem=recv_sem, device_id=device, device_id_type=MESH
        )
        copy.start()
        return copy

    sends = []
    meta_copies = [
        send(meta_out, meta.at[me], meta_send.at[j - 1], meta_recv.at[j - 1], group[j]) for j in range(1, SCAN)
    ]
    near_copies = []
    for k in range(S):
        near_copies.append(
            [
                send(object_ref.at[:, k], obj.at[0, :, k], near_send.at[k, 0], near_recv.at[k, 0], around[1]),
                send(object_ref.at[:, k], obj.at[2, :, k], near_send.at[k, 1], near_recv.at[k, 1], around[-1]),
            ]
        )
    locals_[1].wait()
    intensity = probe[0] * probe[0] + probe[1] * probe[1]
    step = 0.5 / (jnp.max(intensity, keepdims=True) + 1e-06)

    for copy in meta_copies:
        copy.wait_recv()
    seen = [[meta[s, f : f + 1, :] for f in range(5)] for s in range(SCAN)]
    count = jnp.zeros((ROWS, W), jnp.int32)
    first_row = first_col = second_row = second_col = empty_rank = count
    empties = jnp.zeros((1, W), jnp.int32)
    for s in range(SCAN):
        here = row == s
        count = jnp.where(here, seen[s][0], count)
        first_row = jnp.where(here, seen[s][1], first_row)
        first_col = jnp.where(here, seen[s][2], first_col)
        empty_rank = jnp.where(here, empties, empty_rank)
        empties = empties + jnp.where(seen[s][0] == 0, 1, 0)
    takes = []
    doubles = jnp.zeros((1, W), jnp.int32)
    for s in range(SCAN):
        match = jnp.where((seen[s][0] == 2) & (doubles == empty_rank) & (count == 0), 1, 0)
        doubles = doubles + jnp.where(seen[s][0] == 2, 1, 0)
        jobs[2 + s] = match
        second_row = jnp.where(match == 1, seen[s][3], second_row)
        second_col = jnp.where(match == 1, seen[s][4], second_col)
    jobs[0] = jnp.where(count == 0, second_row, first_row)
    jobs[1] = jnp.where(count == 0, second_col, first_col)

    def masks(s):
        wide = jnp.broadcast_to(jobs[1, pl.ds(s, 1), :], (ROWS, W))
        tall = jnp.broadcast_to(jobs[0, pl.ds(s, 1), :], (ROWS, W))
        return lane >= wide, tall

    job_masks = [masks(group[j][1]) for j in range(SCAN)]
    before_masks = [me * ROWS + row >= tall for _, tall in job_masks]

    def gather(it, k):
        bands = [[[obj[b, p, k, :, h * W : (h + 1) * W] for h in range(2)] for p in range(2)] for b in range(3)]
        for j in range(SCAN):
            left_part = job_masks[j][0]
            for p in range(2):
                prev, own, after = [jnp.where(left_part, bands[b][p][0], bands[b][p][1]) for b in range(3)]
                merged = jnp.where(before_masks[j], prev, after)
                if j == 0:
                    patch[it, k, p, 0, my_rows, :] = merged
                    patch[it, k, p, 1, my_rows, :] = own
                else:
                    gather_out[it, k, j - 1, p, 0] = merged
                    gather_out[it, k, j - 1, p, 1] = own
            if j:
                send(
                    gather_out.at[it, k, j - 1],
                    patch.at[it, k, :, :, my_rows, :],
                    gather_send.at[it, k, j - 1],
                    gather_recv.at[it, k, j - 1],
                    group[j],
                )

    def gather_wait(it, k):
        for j in range(1, SCAN):
            pltpu.make_async_remote_copy(
                src_ref=gather_out.at[it, k, j - 1],
                dst_ref=patch.at[it, k, :, :, pl.ds(pl.multiple_of(source[j] * ROWS, ROWS), ROWS), :],
                send_sem=gather_send.at[it, k, j - 1],
                recv_sem=gather_recv.at[it, k, j - 1],
                device_id=group[j],
                device_id_type=MESH,
            ).wait_recv()

    locals_[0].wait()
    for k in range(S):
        for copy in near_copies[k]:
            copy.wait_recv()
        gather(0, k)
    meas_copies = [
        send(measured_ref.at[1], meas_in.at[j - 1], meas_send.at[j - 1], meas_recv.at[j - 1], group[j])
        for j in range(1, SCAN)
    ]

    my_row = jobs[0, pl.ds(me, 1), :]
    my_col = jobs[1, pl.ds(me, 1), :]
    for p in range(2):
        shift_probe[p] = shifted(shifted(probe[p], my_row, 0), my_col, 1)
    locals_[2].wait()
    locals_[3].wait()
    locals_[4].wait()

    for it in range(ITERS):
        final = it == ITERS - 1

        def fetch(k):
            gather_wait(it, k)
            return patch[it, k, 0].reshape(W, W), patch[it, k, 1].reshape(W, W)

        def reduce_send_all(k, value):
            for p in range(2):
                grad[it, k, p] = value[p].reshape(2, W // 2, W)
            for j in range(1, SCAN):
                rows = pl.ds(pl.multiple_of(group[j][1] * ROWS, ROWS), ROWS)
                send(
                    grad.at[it, k, :, :, rows, :],
                    grad_in.at[it, k, j - 1],
                    reduce_send.at[it, k, j - 1],
                    reduce_recv.at[it, k, j - 1],
                    group[j],
                )

        shone = (shift_probe[0], shift_probe[1])
        arrived = [shone]
        patches = [fetch(0)]
        wave = mul(shone, patches[0])
        for k in range(1, S):
            arrived.append(sandwich(*wave, left, right, PROP))
            patches.append(fetch(k))
            wave = mul(arrived[k], patches[k])
        far = sandwich(*wave, left, right, DFT)
        if it == 0:
            value = meas[...]
            for j in range(1, SCAN):
                meas_copies[j - 1].wait_recv()
                take = jobs[pl.ds(2 + source[j], 1), pl.ds(me, 1), :].reshape(1, W)
                value = jnp.where(take == 1, meas_in[j - 1], value)
            meas[...] = value
        ratio = meas[...] * lax.rsqrt(jnp.maximum(far[0] * far[0] + far[1] * far[1], 0.04))
        back = sandwich(far[0] - ratio * far[0], far[1] - ratio * far[1], left, right, DFT_C)
        for k in range(S - 1, 0, -1):
            reduce_send_all(k, mul_conj(arrived[k], back))
            back = sandwich(*mul_conj(patches[k], back), left, right, PROP_C)
        reduce_send_all(0, mul_conj(shone, back))

        for k in range(S - 1, -1, -1):
            zero = jnp.zeros((ROWS, W), F32)
            total = [[[zero, zero] for p in range(2)] for b in range(3)]
            for j in range(SCAN):
                sender = lax.rem(me + SCAN - j, SCAN)
                left_part, tall = masks(sender)
                before = me * ROWS + row >= tall
                if j:
                    pltpu.make_async_remote_copy(
                        src_ref=grad.at[it, k, :, :, my_rows, :],
                        dst_ref=grad_in.at[it, k, j - 1],
                        send_sem=reduce_send.at[it, k, j - 1],
                        recv_sem=reduce_recv.at[it, k, j - 1],
                        device_id=group[j],
                        device_id_type=MESH,
                    ).wait_recv()
                for p in range(2):
                    if j:
                        merged, own = grad_in[it, k, j - 1, p, 0], grad_in[it, k, j - 1, p, 1]
                    else:
                        merged, own = grad[it, k, p, 0, my_rows, :], grad[it, k, p, 1, my_rows, :]
                    for b, term in ((0, jnp.where(before, merged, 0.0)), (1, own), (2, jnp.where(before, 0.0, merged))):
                        total[b][p][0] = total[b][p][0] + jnp.where(left_part, term, 0.0)
                        total[b][p][1] = total[b][p][1] + jnp.where(left_part, 0.0, term)
            for b in range(3):
                for p in range(2):
                    for h in range(2):
                        part[it, k, b, p, :, h * W : (h + 1) * W] = total[b][p][h]
            if final:
                for n, (d, b) in enumerate(((1, 2), (-1, 0))):
                    send(part.at[it, k, b], last_in.at[k, n], last_send.at[k, n], last_recv.at[k, n], around[d])
            else:
                for n, (d, b, w) in enumerate(((1, 1, 2), (-1, 0, 2), (2, 2, 1), (-2, 0, 1))):
                    send(
                        part.at[it, k, pl.ds(b, w)],
                        cross_in.at[k, pl.ds((0, 2, 4, 5)[n], w)],
                        cross_send.at[k, n],
                        cross_recv.at[k, n],
                        around[d],
                    )

        for k in range(S - 1, -1, -1):
            if final:
                for n, (d, b) in enumerate(((1, 2), (-1, 0))):
                    pltpu.make_async_remote_copy(
                        src_ref=part.at[it, k, b], dst_ref=last_in.at[k, n], send_sem=last_send.at[k, n],
                        recv_sem=last_recv.at[k, n], device_id=around[d], device_id_type=MESH,
                    ).wait_recv()
                for p in range(2):
                    gradient = part[it, k, 1, p] + last_in[k, 0, p] + last_in[k, 1, p]
                    out_ref[p, k] = obj[1, p, k] - step * gradient
            else:
                for n, (d, b, w) in enumerate(((1, 1, 2), (-1, 0, 2), (2, 2, 1), (-2, 0, 1))):
                    pltpu.make_async_remote_copy(
                        src_ref=part.at[it, k, pl.ds(b, w)], dst_ref=cross_in.at[k, pl.ds((0, 2, 4, 5)[n], w)],
                        send_sem=cross_send.at[k, n], recv_sem=cross_recv.at[k, n], device_id=around[d],
                        device_id_type=MESH,
                    ).wait_recv()
                for b, (one, two) in enumerate(((0, 4), (1, 2), (3, 5))):
                    for p in range(2):
                        gradient = part[it, k, b, p] + cross_in[k, one, p] + cross_in[k, two, p]
                        obj[b, p, k] = obj[b, p, k] - step * gradient
                gather(it + 1, k)

    for copy in meta_copies + meas_copies + [copy for pair in near_copies for copy in pair]:
        copy.wait_send()
    for it in range(ITERS):
        for k in range(S):
            for j in range(1, SCAN):
                pltpu.make_async_copy(
                    gather_out.at[it, k, j - 1], gather_out.at[it, k, j - 1], gather_send.at[it, k, j - 1]
                ).wait()
                pltpu.make_async_copy(
                    grad_in.at[it, k, j - 1], grad_in.at[it, k, j - 1], reduce_send.at[it, k, j - 1]
                ).wait()
    for k in range(S):
        for n, w in enumerate((2, 2, 1, 1)):
            pltpu.make_async_copy(part.at[0, k, pl.ds(0, w)], part.at[0, k, pl.ds(0, w)], cross_send.at[k, n]).wait()
        for n in range(2):
            pltpu.make_async_copy(part.at[1, k, 0], part.at[1, k, 0], last_send.at[k, n]).wait()


def body(tiles, object_slices, probe_wave, offsets, counts, measured):
    lefts, rights = tables()
    peers = SCAN - 1
    dma = pltpu.SemaphoreType.DMA
    any_space = pl.BlockSpec(memory_space=pl.ANY)
    smem = pl.BlockSpec(memory_space=pltpu.SMEM)
    scratch = [
        pltpu.VMEM((3, 2, S, ROWS, 2 * W), F32),
        pltpu.VMEM((2, W, W), F32),
        pltpu.VMEM((2, W, W), F32),
        pltpu.VMEM((W, W), F32),
        pltpu.VMEM((peers, W, W), F32),
        pltpu.VMEM(lefts.shape, BF16),
        pltpu.VMEM(rights.shape, BF16),
        pltpu.VMEM((ROWS, W), jnp.int32),
        pltpu.VMEM((SCAN, ROWS, W), jnp.int32),
        pltpu.VMEM((2 + SCAN, ROWS, W), jnp.int32),
        pltpu.VMEM((ITERS, S, 2, 2, W // 2, W), F32),
        pltpu.VMEM((ITERS, S, peers, 2, 2, ROWS, W), F32),
        pltpu.VMEM((ITERS, S, 2, 2, W // 2, W), F32),
        pltpu.VMEM((ITERS, S, peers, 2, 2, ROWS, W), F32),
        pltpu.VMEM((ITERS, S, 3, 2, ROWS, 2 * W), F32),
        pltpu.VMEM((S, 6, 2, ROWS, 2 * W), F32),
        pltpu.VMEM((S, 2, 2, ROWS, 2 * W), F32),
    ]
    for shape in ((S, 2), (peers,), (peers,), (ITERS, S, peers), (ITERS, S, peers), (S, 4), (S, 2)):
        scratch += [dma(shape), dma(shape)]
    scratch.append(dma((5,)))
    return pl.pallas_call(
        functools.partial(kernel, tiles),
        out_shape=jax.ShapeDtypeStruct(object_slices.shape, F32),
        in_specs=[smem, smem] + [any_space] * 5,
        out_specs=pl.BlockSpec(memory_space=pltpu.VMEM),
        scratch_shapes=scratch,
        compiler_params=pltpu.CompilerParams(
            collective_id=0, has_side_effects=True, vmem_limit_bytes=VMEM_BYTES
        ),
    )(offsets, counts, object_slices, probe_wave, measured, jnp.asarray(lefts), jnp.asarray(rights))


def solution(mesh):
    placed = (
        P(None, None, ("tile", "scan"), None),
        P(),
        P(("tile", "scan"), None),
        P(("tile", "scan")),
        P(("tile", "scan"), None, None),
    )
    return jax.shard_map(
        functools.partial(body, mesh.shape["tile"]),
        mesh=mesh,
        in_specs=placed,
        out_specs=P(None, None, ("tile", "scan"), None),
        check_vma=False,
    )
```

```python
import functools

import jax
import jax.numpy as jnp
import ml_dtypes
import numpy as np
from jax import lax
from jax.experimental import pallas as pl
from jax.experimental.pallas import tpu as pltpu
from jax.sharding import PartitionSpec as P


ITERS = 2
S = 4
W = 128
SCAN = 8
ROWS = 8
PROP, PROP_C, DFT, DFT_C = range(4)
MESH = pl.DeviceIdType.MESH
F32 = jnp.float32
BF16 = jnp.bfloat16
VMEM_BYTES = 60 * 2**20


def tables():
    n = np.arange(W)
    dft = np.exp(-2j * np.pi * (n[:, None] * n[None, :] % W) / W) / np.sqrt(W)
    freq = (n + W // 2) % W - W // 2
    prop = np.conj(dft) @ (np.exp(-1j * np.pi * freq * freq / (2.0 * W))[:, None] * dft)
    lefts, rights = [], []
    for m in (prop, np.conj(prop), dft, np.conj(dft)):
        right = np.block([[m.real, m.imag], [-m.imag, m.real]])
        left = np.block([[m.real, -m.imag], [m.imag, m.real]])
        for big, out, axis in ((right, rights, 0), (left, lefts, 1)):
            high = big.astype(ml_dtypes.bfloat16)
            low = (big - high.astype(np.float64)).astype(ml_dtypes.bfloat16)
            out.append(np.concatenate([high, high, low], axis=axis))
    return np.stack(lefts), np.stack(rights)


def halves(value):
    high = value.astype(BF16)
    return high, (value - high.astype(F32)).astype(BF16)


def sandwich(re, im, left_ref, right_ref, which):
    high, low = halves(jnp.concatenate([re, im], axis=0))
    mid = jnp.dot(left_ref[which], jnp.concatenate([high, low, high], axis=0), preferred_element_type=F32)
    high, low = halves(jnp.concatenate([mid[:W], mid[W:]], axis=1))
    out = jnp.dot(jnp.concatenate([high, low, high], axis=1), right_ref[which], preferred_element_type=F32)
    return out[:, :W], out[:, W:]


def mul(a, b):
    return a[0] * b[0] - a[1] * b[1], a[0] * b[1] + a[1] * b[0]


def mul_conj(a, b):
    return a[0] * b[0] + a[1] * b[1], a[0] * b[1] - a[1] * b[0]


def shifted(value, amount, axis):
    for bit in range(7):
        moved = pltpu.roll(value, 1 << bit, axis)
        value = jnp.where(lax.rem(lax.div(amount, 1 << bit), 2) == 1, moved, value)
    return value

class Links:
    def __init__(self, sems):
        self.sems = sems
        self.started = []
        self.open = {}

    def send(self, name, index, src, dst, device, own=None):
        send_sem, recv_sem = self.sems[name]
        copy = pltpu.make_async_remote_copy(
            src_ref=src, dst_ref=dst, send_sem=send_sem.at[index], recv_sem=recv_sem.at[index], device_id=device,
            device_id_type=MESH,
        )
        if own is None:
            copy.start()
        else:
            pl.when(own)(lambda: pltpu.make_async_copy(src, dst, recv_sem.at[index]).start())
            pl.when(jnp.logical_not(own))(copy.start)
        self.started.append((copy, own))
        self.open[name, index] = copy

    def receive(self, name, index, dst=None):
        copy = self.open.pop((name, index))
        if dst is not None:
            copy = pltpu.make_async_remote_copy(
                src_ref=copy.src_ref, dst_ref=dst, send_sem=copy.src_sem, recv_sem=copy.dst_sem,
                device_id=copy.device_id, device_id_type=MESH,
            )
        copy.wait_recv()

    def finish(self):
        for copy, own in self.started:
            if own is None:
                copy.wait_send()
        if any(own is not None for _, own in self.started):
            own = [own for _, own in self.started if own is not None][0]

            @pl.when(jnp.logical_not(own))
            def _():
                for copy, own in self.started:
                    if own is not None:
                        copy.wait_send()


CROSS = ((1, 1, 2, 0), (-1, 0, 2, 2), (2, 2, 1, 4), (-2, 0, 1, 5))
LAST = ((1, 2), (-1, 0))


def twin(tile, scan):
    core, half = lax.rem(tile, 2), lax.div(scan, 4)
    return tile - core + half, lax.rem(scan, 4) + 4 * core


def kernel(
    tiles, names, offsets_hbm, counts_hbm, object_hbm, probe_hbm, measured_hbm, lefts_hbm, rights_hbm, out_ref,
    offsets_ref, counts_ref, obj, obj_work, out_base, probe, shift_probe, meas, meas_in, left, right, meta_out,
    meta_own, meta_work, jobs_own, jobs_work, patch, gather_out, grad, grad_in, part, cross_in, last_in, local_sem,
    *sems,
):
    links = Links({name: (sems[2 * i], sems[2 * i + 1]) for i, name in enumerate(names)})
    tile = lax.axis_index("tile")
    me = lax.axis_index("scan")
    region, member = twin(tile, me)
    same = region == tile

    def ring(first, j):
        return lax.rem(first + j + SCAN, SCAN)

    owners = [(tile, ring(me, j)) for j in range(SCAN)]
    workers = [twin(tile, ring(me, j)) for j in range(SCAN)]
    members = [twin(region, ring(member, j)) for j in range(SCAN)]
    region_owners = [(region, ring(member, j)) for j in range(SCAN)]
    near = {d: (lax.rem(tile + d + tiles, tiles), me) for d in (-1, 1)}
    around = {d: twin(lax.rem(region + d + tiles, tiles), member) for d in (-2, -1, 1, 2)}

    def rows_of(s):
        return pl.ds(pl.multiple_of(s * ROWS, ROWS), ROWS)

    barrier = pltpu.get_barrier_semaphore()
    others = owners[1:] + workers[1:] + members[1:] + region_owners[1:] + list(near.values()) + list(around.values())
    for device in others:
        pl.semaphore_signal(barrier, inc=1, device_id=device, device_id_type=MESH)

    @pl.when(jnp.logical_not(same))
    def _():
        pl.semaphore_signal(barrier, inc=1, device_id=workers[0], device_id_type=MESH)

    local = {}
    for n, (name, src, dst) in enumerate(
        (
            ("offsets", offsets_hbm, offsets_ref),
            ("counts", counts_hbm, counts_ref),
            ("probe", probe_hbm, probe),
            ("object", object_hbm, obj.at[1]),
            ("lefts", lefts_hbm, left),
            ("rights", rights_hbm, right),
        )
    ):
        local[name] = pltpu.make_async_copy(src, dst, local_sem.at[n])
        local[name].start()

    row = lax.broadcasted_iota(jnp.int32, (ROWS, W), 0)
    lane = lax.broadcasted_iota(jnp.int32, (ROWS, W), 1)
    local.pop("offsets").wait()
    local.pop("counts").wait()
    fields = [counts_ref[0], offsets_ref[0, 0], offsets_ref[0, 1], offsets_ref[1, 0], offsets_ref[1, 1]]
    packed = jnp.zeros((ROWS, W), jnp.int32)
    for f, field in enumerate(fields):
        packed = jnp.where(row == f, field, packed)
    meta_out[...] = packed
    meta_own[me] = packed

    pl.semaphore_wait(barrier, len(others) + jnp.where(same, 0, 1))

    for j in range(1, SCAN):
        links.send("meta_own", (j - 1,), meta_out, meta_own.at[me], owners[j])
    for j in range(SCAN):
        links.send("meta_work", (j,), meta_out, meta_work.at[me], workers[j], None if j else same)
    for k in range(S):
        links.send("near", (k, 0), object_hbm.at[:, k], obj.at[0, :, k], near[1])
        links.send("near", (k, 1), object_hbm.at[:, k], obj.at[2, :, k], near[-1])
    links.send("meas", (0,), measured_hbm.at[0], meas_in.at[0], workers[0], same)
    for j in range(1, SCAN):
        links.send("meas", (j,), measured_hbm.at[1], meas_in.at[j], workers[j])
    local.pop("probe").wait()
    intensity = probe[0] * probe[0] + probe[1] * probe[1]
    step = 0.5 / (jnp.max(intensity, keepdims=True) + 1e-06)

    def assign(meta, jobs):
        seen = [[meta[s, f : f + 1, :] for f in range(5)] for s in range(SCAN)]
        count = jnp.zeros((ROWS, W), jnp.int32)
        first_row = first_col = second_row = second_col = empty_rank = count
        empties = jnp.zeros((1, W), jnp.int32)
        for s in range(SCAN):
            here = row == s
            count = jnp.where(here, seen[s][0], count)
            first_row = jnp.where(here, seen[s][1], first_row)
            first_col = jnp.where(here, seen[s][2], first_col)
            empty_rank = jnp.where(here, empties, empty_rank)
            empties = empties + jnp.where(seen[s][0] == 0, 1, 0)
        doubles = jnp.zeros((1, W), jnp.int32)
        for s in range(SCAN):
            match = jnp.where((seen[s][0] == 2) & (doubles == empty_rank) & (count == 0), 1, 0)
            doubles = doubles + jnp.where(seen[s][0] == 2, 1, 0)
            jobs[2 + s] = match
            second_row = jnp.where(match == 1, seen[s][3], second_row)
            second_col = jnp.where(match == 1, seen[s][4], second_col)
        jobs[0] = jnp.where(count == 0, second_row, first_row)
        jobs[1] = jnp.where(count == 0, second_col, first_col)

    def masks(jobs, worker, place):
        wide = jnp.broadcast_to(jobs[1, pl.ds(worker, 1), :], (ROWS, W))
        tall = jnp.broadcast_to(jobs[0, pl.ds(worker, 1), :], (ROWS, W))
        return lane >= wide, place * ROWS + row >= tall

    def gather(it, k):
        jobs, bands_ref, place, targets = (
            (jobs_work, obj_work, member, members) if it else (jobs_own, obj, me, workers)
        )
        bands = [[[bands_ref[b, p, k, :, h * W : (h + 1) * W] for h in range(2)] for p in range(2)] for b in range(3)]
        for j in range(SCAN):
            left_part, before = masks(jobs, ring(place, j), place)
            for p in range(2):
                prev, own, after = [jnp.where(left_part, bands[b][p][0], bands[b][p][1]) for b in range(3)]
                merged = jnp.where(before, prev, after)
                if j == 0 and it:
                    patch[it, k, p, 0, rows_of(place), :] = merged
                    patch[it, k, p, 1, rows_of(place), :] = own
                else:
                    gather_out[it, k, j, p, 0] = merged
                    gather_out[it, k, j, p, 1] = own
            if j or not it:
                links.send(
                    "gather", (it, k, j), gather_out.at[it, k, j], patch.at[it, k, :, :, rows_of(place), :], targets[j],
                    None if j else same,
                )

    for j in range(1, SCAN):
        links.receive("meta_own", (j - 1,), meta_own.at[ring(me, -j)])
    assign(meta_own, jobs_own)
    local.pop("object").wait()
    for k in range(S):
        links.receive("near", (k, 0))
        links.receive("near", (k, 1))
        gather(0, k)
    links.send("replica", (0,), obj, obj_work, workers[0], same)

    for j in range(SCAN):
        links.receive("meta_work", (j,), meta_work.at[ring(member, -j)])
    assign(meta_work, jobs_work)
    my_row = jobs_work[0, pl.ds(member, 1), :]
    my_col = jobs_work[1, pl.ds(member, 1), :]
    for p in range(2):
        shift_probe[p] = shifted(shifted(probe[p], my_row, 0), my_col, 1)
    for name in ("lefts", "rights"):
        local.pop(name).wait()

    for it in range(ITERS):
        final = it == ITERS - 1

        def fetch(k):
            for j in range(1 if it else 0, SCAN):
                links.receive("gather", (it, k, j), patch.at[it, k, :, :, rows_of(ring(member, -j)), :])
            return patch[it, k, 0].reshape(W, W), patch[it, k, 1].reshape(W, W)

        def reduce_start(k, value):
            for p in range(2):
                grad[it, k, p] = value[p].reshape(2, W // 2, W)
            for j in range(0 if final else 1, SCAN):
                links.send(
                    "reduce", (it, k, j), grad.at[it, k, :, :, rows_of(ring(member, j)), :], grad_in.at[it, k, j],
                    region_owners[j] if final else members[j], None if j else same,
                )

        def reduce_end(k):
            jobs, place = (jobs_own, me) if final else (jobs_work, member)
            zero = jnp.zeros((ROWS, W), F32)
            total = [[[zero, zero] for p in range(2)] for b in range(3)]
            for j in range(SCAN):
                left_part, before = masks(jobs, ring(place, -j), place)
                if j or final:
                    links.receive("reduce", (it, k, j))
                for p in range(2):
                    if j or final:
                        merged, own = grad_in[it, k, j, p, 0], grad_in[it, k, j, p, 1]
                    else:
                        merged, own = grad[it, k, p, 0, rows_of(place), :], grad[it, k, p, 1, rows_of(place), :]
                    for b, term in ((0, jnp.where(before, merged, 0.0)), (1, own), (2, jnp.where(before, 0.0, merged))):
                        total[b][p][0] = total[b][p][0] + jnp.where(left_part, term, 0.0)
                        total[b][p][1] = total[b][p][1] + jnp.where(left_part, 0.0, term)
            for b in range(3):
                for p in range(2):
                    for h in range(2):
                        part[it, k, b, p, :, h * W : (h + 1) * W] = total[b][p][h]

        def pass_on(k):
            reduce_end(k)
            if final:
                for n, (d, b) in enumerate(LAST):
                    links.send("last", (k, n), part.at[it, k, b], last_in.at[k, n], near[d])
            else:
                for n, (d, b, w, at) in enumerate(CROSS):
                    links.send("cross", (k, n), part.at[it, k, pl.ds(b, w)], cross_in.at[k, pl.ds(at, w)], around[d])

        def update(k):
            if final:
                for n in range(len(LAST)):
                    links.receive("last", (k, n))
                for p in range(2):
                    gradient = part[it, k, 1, p] + last_in[k, 0, p] + last_in[k, 1, p]
                    out_ref[p, k] = out_base[p, k] - step * gradient
            else:
                for n in range(len(CROSS)):
                    links.receive("cross", (k, n))
                for b, (one, two) in enumerate(((0, 4), (1, 2), (3, 5))):
                    for p in range(2):
                        gradient = part[it, k, b, p] + cross_in[k, one, p] + cross_in[k, two, p]
                        obj_work[b, p, k] = obj_work[b, p, k] - step * gradient
                gather(it + 1, k)

        shone = (shift_probe[0], shift_probe[1])
        arrived = [shone]
        patches = [fetch(0)]
        wave = mul(shone, patches[0])
        for k in range(1, S):
            arrived.append(sandwich(*wave, left, right, PROP))
            patches.append(fetch(k))
            wave = mul(arrived[k], patches[k])
        far = sandwich(*wave, left, right, DFT)
        if it == 0:
            links.receive("meas", (0,))
            value = meas_in[0]
            for j in range(1, SCAN):
                links.receive("meas", (j,))
                take = jobs_work[pl.ds(2 + ring(member, -j), 1), pl.ds(member, 1), :].reshape(1, W)
                value = jnp.where(take == 1, meas_in[j], value)
            meas[...] = value
        ratio = meas[...] * lax.rsqrt(jnp.maximum(far[0] * far[0] + far[1] * far[1], 0.04))
        back = sandwich(far[0] - ratio * far[0], far[1] - ratio * far[1], left, right, DFT_C)
        for k in range(S - 1, 0, -1):
            reduce_start(k, mul_conj(arrived[k], back))
            back = sandwich(*mul_conj(patches[k], back), left, right, PROP_C)
        reduce_start(0, mul_conj(shone, back))

        pass_on(3)
        pass_on(2)
        links.receive("base" if final else "replica", (0,))
        update(3)
        pass_on(1)
        update(2)
        pass_on(0)
        update(1)
        update(0)
        if not final:
            links.send("base", (0,), obj_work.at[1], out_base, region_owners[0], same)

    links.finish()


def body(tiles, object_slices, probe_wave, offsets, counts, measured):
    lefts, rights = tables()
    dma = pltpu.SemaphoreType.DMA
    hbm = pl.BlockSpec(memory_space=pltpu.HBM)
    scratch = [
        pltpu.SMEM(offsets.shape, jnp.int32),
        pltpu.SMEM(counts.shape, jnp.int32),
        pltpu.VMEM((3, 2, S, ROWS, 2 * W), F32),
        pltpu.VMEM((3, 2, S, ROWS, 2 * W), F32),
        pltpu.VMEM((2, S, ROWS, 2 * W), F32),
        pltpu.VMEM((2, W, W), F32),
        pltpu.VMEM((2, W, W), F32),
        pltpu.VMEM((W, W), F32),
        pltpu.VMEM((SCAN, W, W), F32),
        pltpu.VMEM(lefts.shape, BF16),
        pltpu.VMEM(rights.shape, BF16),
        pltpu.VMEM((ROWS, W), jnp.int32),
        pltpu.VMEM((SCAN, ROWS, W), jnp.int32),
        pltpu.VMEM((SCAN, ROWS, W), jnp.int32),
        pltpu.VMEM((2 + SCAN, ROWS, W), jnp.int32),
        pltpu.VMEM((2 + SCAN, ROWS, W), jnp.int32),
        pltpu.VMEM((ITERS, S, 2, 2, W // 2, W), F32),
        pltpu.VMEM((ITERS, S, SCAN, 2, 2, ROWS, W), F32),
        pltpu.VMEM((ITERS, S, 2, 2, W // 2, W), F32),
        pltpu.VMEM((ITERS, S, SCAN, 2, 2, ROWS, W), F32),
        pltpu.VMEM((ITERS, S, 3, 2, ROWS, 2 * W), F32),
        pltpu.VMEM((S, 6, 2, ROWS, 2 * W), F32),
        pltpu.VMEM((S, 2, 2, ROWS, 2 * W), F32),
        dma((6,)),
    ]
    shapes = {
        "meta_own": (SCAN - 1,),
        "meta_work": (SCAN,),
        "near": (S, 2),
        "meas": (SCAN,),
        "replica": (1,),
        "gather": (ITERS, S, SCAN),
        "reduce": (ITERS, S, SCAN),
        "cross": (S, len(CROSS)),
        "base": (1,),
        "last": (S, len(LAST)),
    }
    for shape in shapes.values():
        scratch += [dma(shape), dma(shape)]
    return pl.pallas_call(
        functools.partial(kernel, tiles, tuple(shapes)),
        out_shape=jax.ShapeDtypeStruct(object_slices.shape, F32),
        in_specs=[hbm] * 7,
        out_specs=pl.BlockSpec(memory_space=pltpu.VMEM),
        scratch_shapes=scratch,
        compiler_params=pltpu.CompilerParams(
            collective_id=0, has_side_effects=True, vmem_limit_bytes=VMEM_BYTES
        ),
    )(offsets, counts, object_slices, probe_wave, measured, jnp.asarray(lefts), jnp.asarray(rights))


def solution(mesh):
    placed = (
        P(None, None, ("tile", "scan"), None),
        P(),
        P(("tile", "scan"), None),
        P(("tile", "scan")),
        P(("tile", "scan"), None, None),
    )
    return jax.shard_map(
        functools.partial(body, mesh.shape["tile"]),
        mesh=mesh,
        in_specs=placed,
        out_specs=P(None, None, ("tile", "scan"), None),
        check_vma=False,
    )
```

```python
import functools

import jax
import jax.numpy as jnp
import ml_dtypes
import numpy as np
from jax import lax
from jax.experimental import pallas as pl
from jax.experimental.pallas import tpu as pltpu
from jax.sharding import PartitionSpec as P


ITERS = 2
S = 4
W = 128
SCAN = 8
ROWS = 8
PROP, PROP_C, DFT, DFT_C = range(4)
MESH = pl.DeviceIdType.MESH
F32 = jnp.float32
BF16 = jnp.bfloat16
VMEM_BYTES = 60 * 2**20


def tables():
    n = np.arange(W)
    dft = np.exp(-2j * np.pi * (n[:, None] * n[None, :] % W) / W) / np.sqrt(W)
    freq = (n + W // 2) % W - W // 2
    prop = np.conj(dft) @ (np.exp(-1j * np.pi * freq * freq / (2.0 * W))[:, None] * dft)
    parts = []
    for part in (prop.real, prop.imag, dft.real, dft.imag):
        high = part.astype(ml_dtypes.bfloat16)
        parts += [high, (part - high.astype(np.float64)).astype(ml_dtypes.bfloat16)]
    return np.stack(parts)


def spread(parts_ref, left_ref, right_ref):
    for which, (first, sign) in enumerate(((0, 1), (0, -1), (4, 1), (4, -1))):
        for place, low in enumerate((0, 0, 1)):
            re = parts_ref[first + low]
            im = parts_ref[first + 2 + low]
            plus, minus = (im, -im) if sign == 1 else (-im, im)
            at = low * 2 * W
            if place:
                left_ref[which, :W, at : at + W] = re
                left_ref[which, :W, at + W : at + 2 * W] = minus
                left_ref[which, W:, at : at + W] = plus
                left_ref[which, W:, at + W : at + 2 * W] = re
            at = place * 2 * W
            right_ref[which, at : at + W, :W] = re
            right_ref[which, at : at + W, W:] = plus
            right_ref[which, at + W : at + 2 * W, :W] = minus
            right_ref[which, at + W : at + 2 * W, W:] = re


def halves(value):
    high = value.astype(BF16)
    return high, (value - high.astype(F32)).astype(BF16)


def sandwich(re, im, left_ref, right_ref, which):
    high, low = halves(jnp.concatenate([re, im], axis=0))
    left = left_ref[which]
    both = jnp.dot(left[:, : 2 * W], jnp.concatenate([high, low], axis=1), preferred_element_type=F32)
    mid = both[:, :W] + both[:, W:] + jnp.dot(left[:, 2 * W :], high, preferred_element_type=F32)
    high, low = halves(jnp.concatenate([mid[:W], mid[W:]], axis=1))
    rows = jnp.concatenate([high, low, high], axis=1)
    right = right_ref[which]
    upper = jnp.dot(rows[: W // 2], right, preferred_element_type=F32)
    lower = jnp.dot(rows[W // 2 :], right, preferred_element_type=F32)
    out = jnp.concatenate([upper, lower], axis=0)
    return out[:, :W], out[:, W:]


def mul(a, b):
    return a[0] * b[0] - a[1] * b[1], a[0] * b[1] + a[1] * b[0]


def mul_conj(a, b):
    return a[0] * b[0] + a[1] * b[1], a[0] * b[1] - a[1] * b[0]


def shifted(value, amount, axis):
    for bit in range(7):
        moved = pltpu.roll(value, 1 << bit, axis)
        value = jnp.where(lax.rem(lax.div(amount, 1 << bit), 2) == 1, moved, value)
    return value

class Links:
    def __init__(self, sems):
        self.sems = sems
        self.started = []
        self.open = {}

    def send(self, name, index, src, dst, device):
        send_sem, recv_sem = self.sems[name]
        copy = pltpu.make_async_remote_copy(
            src_ref=src, dst_ref=dst, send_sem=send_sem.at[index], recv_sem=recv_sem.at[index], device_id=device,
            device_id_type=MESH,
        )
        copy.start()
        self.started.append(copy)
        self.open[name, index] = copy

    def receive(self, name, index, dst=None):
        copy = self.open.pop((name, index))
        if dst is not None:
            copy = pltpu.make_async_remote_copy(
                src_ref=copy.src_ref, dst_ref=dst, send_sem=copy.src_sem, recv_sem=copy.dst_sem,
                device_id=copy.device_id, device_id_type=MESH,
            )
        copy.wait_recv()

    def finish(self):
        for copy in self.started:
            copy.wait_send()


CROSS = ((1, 1, 2, 0), (-1, 0, 2, 2), (2, 2, 1, 4), (-2, 0, 1, 5))
LAST = ((1, 2), (-1, 0))
BITS = (2, 1, 4)


def twin(tile, scan):
    core, half, odd = lax.rem(tile, 2), lax.div(scan, 4), lax.rem(lax.div(tile, 2), 2)
    return tile - core + half + 2 - 4 * odd, lax.rem(scan, 4) + 4 * core


def kernel(
    tiles, names, offsets_hbm, counts_hbm, object_hbm, probe_hbm, measured_hbm, parts_hbm, out_ref,
    offsets_ref, counts_ref, obj, obj_work, out_base, probe, shift_probe, meas, meas_out, meas_in, parts, left, right, meta_out,
    meta_own, meta_work, jobs_own, jobs_work, patch, gather_out, grad, grad_in, part, cross_in, last_in, local_sem,
    *sems,
):
    links = Links({name: (sems[2 * i], sems[2 * i + 1]) for i, name in enumerate(names)})
    tile = lax.axis_index("tile")
    me = lax.axis_index("scan")
    region, member = twin(tile, me)

    def ring(first, j):
        return lax.rem(first + j + SCAN, SCAN)

    owners = [(tile, ring(me, j)) for j in range(SCAN)]
    workers = [twin(tile, ring(me, j)) for j in range(SCAN)]
    members = [twin(region, ring(member, j)) for j in range(SCAN)]
    region_owners = [(region, ring(member, j)) for j in range(SCAN)]
    partners = []
    for bit in BITS:
        upper = lax.rem(lax.div(member, bit), 2)
        partners.append(twin(region, member + bit - 2 * bit * upper))
    near = {d: (lax.rem(tile + d + tiles, tiles), me) for d in (-1, 1)}
    around = {d: twin(lax.rem(region + d + tiles, tiles), member) for d in (-2, -1, 1, 2)}

    def rows_of(s):
        return pl.ds(pl.multiple_of(s * ROWS, ROWS), ROWS)

    local = {}
    for n, (name, src, dst) in enumerate(
        (
            ("offsets", offsets_hbm, offsets_ref),
            ("counts", counts_hbm, counts_ref),
            ("probe", probe_hbm, probe),
            ("object", object_hbm, obj.at[1]),
            ("parts", parts_hbm, parts),
        )
    ):
        local[name] = pltpu.make_async_copy(src, dst, local_sem.at[n])
        local[name].start()

    barrier = pltpu.get_barrier_semaphore()
    others = owners[1:] + workers + members[1:] + region_owners + list(near.values()) + list(around.values())
    for device in others:
        pl.semaphore_signal(barrier, inc=1, device_id=device, device_id_type=MESH)

    row = lax.broadcasted_iota(jnp.int32, (ROWS, W), 0)
    lane = lax.broadcasted_iota(jnp.int32, (ROWS, W), 1)
    local.pop("offsets").wait()
    local.pop("counts").wait()
    fields = [counts_ref[0], offsets_ref[0, 0], offsets_ref[0, 1], offsets_ref[1, 0], offsets_ref[1, 1]]
    packed = jnp.zeros((ROWS, W), jnp.int32)
    for f, field in enumerate(fields):
        packed = jnp.where(row == f, field, packed)
    meta_out[...] = packed
    meta_own[me] = packed

    pl.semaphore_wait(barrier, len(others))

    for j in range(1, SCAN):
        links.send("meta_own", (j - 1,), meta_out, meta_own.at[me], owners[j])
    for j in range(SCAN):
        links.send("meta_work", (j,), meta_out, meta_work.at[me], workers[j])
    for k in range(S):
        links.send("near", (k, 0), object_hbm.at[:, k], obj.at[0, :, k], near[1])
        links.send("near", (k, 1), object_hbm.at[:, k], obj.at[2, :, k], near[-1])
    links.send("meas", (0,), measured_hbm, meas, workers[0])
    local.pop("probe").wait()
    intensity = probe[0] * probe[0] + probe[1] * probe[1]
    step = 0.5 / (jnp.max(intensity, keepdims=True) + 1e-06)
    local.pop("parts").wait()
    spread(parts, left, right)

    def partner(value, bit):
        upper = lax.rem(lax.div(row, bit), 2) == 1
        if bit == SCAN // 2:
            return pltpu.roll(value, bit, 0)
        return jnp.where(upper, pltpu.roll(value, bit, 0), pltpu.roll(value, SCAN - bit, 0))

    def assign(meta, jobs):
        fields = []
        for f in range(5):
            field = jnp.zeros((ROWS, W), jnp.int32)
            for s in range(SCAN):
                field = jnp.where(row == s, meta[s, f : f + 1, :], field)
            fields.append(field)
        count, lower, upper = fields[0], fields[1:3], fields[3:5]
        for n, bit in enumerate(BITS):
            rest = BITS[n + 1 :]
            total = count
            for other in rest:
                total = total + partner(total, other)
            excess = total - partner(total, bit)
            eager = jnp.where(count > partner(count, bit), 1, 0)
            rank = jnp.zeros((ROWS, W), jnp.int32)
            ahead = eager
            for other in rest:
                rank = rank + jnp.where(lax.rem(lax.div(row, other), 2) == 1, partner(ahead, other), 0)
                ahead = ahead + partner(ahead, other)
            give = jnp.where((eager == 1) & (2 * rank < excess), 1, 0)
            take = partner(give, bit)
            jobs[2 + n] = count
            jobs[5 + n] = take
            for i in range(2):
                handed = partner(jnp.where(count == 2, upper[i], lower[i]), bit)
                lower[i] = jnp.where((take == 1) & (count == 0), handed, lower[i])
                upper[i] = jnp.where((take == 1) & (count == 1), handed, upper[i])
            count = count + take - give
        jobs[0] = lower[0]
        jobs[1] = lower[1]

    def hand_over(n):
        count = jobs_work[2 + n, pl.ds(member, 1), :]
        meas_out[n] = jnp.where(count == 2, meas[1], meas[0])
        links.send("hand", (n,), meas_out.at[n], meas_in.at[n], partners[n])

    def take_over(n):
        links.receive("hand", (n,))
        count = jobs_work[2 + n, pl.ds(member, 1), :]
        take = jobs_work[5 + n, pl.ds(member, 1), :]
        for i in range(2):
            meas[i] = jnp.where((take == 1) & (count == i), meas_in[n], meas[i])

    def masks(jobs, worker, place):
        wide = jnp.broadcast_to(jobs[1, pl.ds(worker, 1), :], (ROWS, W))
        tall = jnp.broadcast_to(jobs[0, pl.ds(worker, 1), :], (ROWS, W))
        return lane >= wide, place * ROWS + row >= tall

    def gather(it, k):
        jobs, bands_ref, place, targets = (
            (jobs_work, obj_work, member, members) if it else (jobs_own, obj, me, workers)
        )
        bands = [[[bands_ref[b, p, k, :, h * W : (h + 1) * W] for h in range(2)] for p in range(2)] for b in range(3)]
        for j in range(SCAN):
            left_part, before = masks(jobs, ring(place, j), place)
            for p in range(2):
                prev, own, after = [jnp.where(left_part, bands[b][p][0], bands[b][p][1]) for b in range(3)]
                merged = jnp.where(before, prev, after)
                if j == 0 and it:
                    patch[it, k, p, 0, rows_of(place), :] = merged
                    patch[it, k, p, 1, rows_of(place), :] = own
                else:
                    gather_out[it, k, j, p, 0] = merged
                    gather_out[it, k, j, p, 1] = own
            if j or not it:
                links.send(
                    "gather", (it, k, j), gather_out.at[it, k, j], patch.at[it, k, :, :, rows_of(place), :], targets[j]
                )

    for j in range(1, SCAN):
        links.receive("meta_own", (j - 1,), meta_own.at[ring(me, -j)])
    assign(meta_own, jobs_own)
    local.pop("object").wait()
    for k in range(S):
        links.receive("near", (k, 0))
        links.receive("near", (k, 1))
        gather(0, k)
        if k == 0:
            for j in range(SCAN):
                links.receive("meta_work", (j,), meta_work.at[ring(member, -j)])
            assign(meta_work, jobs_work)
            links.receive("meas", (0,))
            hand_over(0)

    my_row = jobs_work[0, pl.ds(member, 1), :]
    my_col = jobs_work[1, pl.ds(member, 1), :]
    for p in range(2):
        shift_probe[p] = shifted(shifted(probe[p], my_row, 0), my_col, 1)
    take_over(0)
    hand_over(1)
    links.send("replica", (0,), obj, obj_work, workers[0])

    for it in range(ITERS):
        final = it == ITERS - 1

        def fetch(k):
            for j in range(1 if it else 0, SCAN):
                links.receive("gather", (it, k, j), patch.at[it, k, :, :, rows_of(ring(member, -j)), :])
            return patch[it, k, 0].reshape(W, W), patch[it, k, 1].reshape(W, W)

        def reduce_start(k, value):
            for p in range(2):
                grad[it, k, p] = value[p].reshape(2, W // 2, W)
            for j in range(0 if final else 1, SCAN):
                links.send(
                    "reduce", (it, k, j), grad.at[it, k, :, :, rows_of(ring(member, j)), :], grad_in.at[it, k, j],
                    region_owners[j] if final else members[j],
                )

        def reduce_end(k):
            jobs, place = (jobs_own, me) if final else (jobs_work, member)
            zero = jnp.zeros((ROWS, W), F32)
            total = [[[zero, zero] for p in range(2)] for b in range(3)]
            for j in range(SCAN):
                left_part, before = masks(jobs, ring(place, -j), place)
                if j or final:
                    links.receive("reduce", (it, k, j))
                for p in range(2):
                    if j or final:
                        merged, own = grad_in[it, k, j, p, 0], grad_in[it, k, j, p, 1]
                    else:
                        merged, own = grad[it, k, p, 0, rows_of(place), :], grad[it, k, p, 1, rows_of(place), :]
                    for b, term in ((0, jnp.where(before, merged, 0.0)), (1, own), (2, jnp.where(before, 0.0, merged))):
                        total[b][p][0] = total[b][p][0] + jnp.where(left_part, term, 0.0)
                        total[b][p][1] = total[b][p][1] + jnp.where(left_part, 0.0, term)
            for b in range(3):
                for p in range(2):
                    for h in range(2):
                        part[it, k, b, p, :, h * W : (h + 1) * W] = total[b][p][h]

        def pass_on(k):
            reduce_end(k)
            if final:
                for n, (d, b) in enumerate(LAST):
                    links.send("last", (k, n), part.at[it, k, b], last_in.at[k, n], near[d])
            else:
                for n, (d, b, w, at) in enumerate(CROSS):
                    links.send("cross", (k, n), part.at[it, k, pl.ds(b, w)], cross_in.at[k, pl.ds(at, w)], around[d])

        def update(k):
            if final:
                for n in range(len(LAST)):
                    links.receive("last", (k, n))
                for p in range(2):
                    gradient = part[it, k, 1, p] + last_in[k, 0, p] + last_in[k, 1, p]
                    out_ref[p, k] = out_base[p, k] - step * gradient
            else:
                for n in range(len(CROSS)):
                    links.receive("cross", (k, n))
                for b, (one, two) in enumerate(((0, 4), (1, 2), (3, 5))):
                    for p in range(2):
                        gradient = part[it, k, b, p] + cross_in[k, one, p] + cross_in[k, two, p]
                        obj_work[b, p, k] = obj_work[b, p, k] - step * gradient
                gather(it + 1, k)

        shone = (shift_probe[0], shift_probe[1])
        arrived = [shone]
        patches = [fetch(0)]
        wave = mul(shone, patches[0])
        for k in range(1, S):
            arrived.append(sandwich(*wave, left, right, PROP))
            patches.append(fetch(k))
            if it == 0 and k == 1:
                take_over(1)
                hand_over(2)
            wave = mul(arrived[k], patches[k])
        far = sandwich(*wave, left, right, DFT)
        if it == 0:
            take_over(2)
        ratio = meas[0] * lax.rsqrt(jnp.maximum(far[0] * far[0] + far[1] * far[1], 0.04))
        back = sandwich(far[0] - ratio * far[0], far[1] - ratio * far[1], left, right, DFT_C)
        for k in range(S - 1, 0, -1):
            reduce_start(k, mul_conj(arrived[k], back))
            back = sandwich(*mul_conj(patches[k], back), left, right, PROP_C)
        reduce_start(0, mul_conj(shone, back))

        pass_on(3)
        pass_on(2)
        pass_on(1)
        links.receive("base" if final else "replica", (0,))
        update(3)
        pass_on(0)
        update(2)
        update(1)
        update(0)
        if not final:
            links.send("base", (0,), obj_work.at[1], out_base, region_owners[0])

    links.finish()


def body(tiles, object_slices, probe_wave, offsets, counts, measured):
    parts = tables()
    dma = pltpu.SemaphoreType.DMA
    hbm = pl.BlockSpec(memory_space=pltpu.HBM)
    scratch = [
        pltpu.SMEM(offsets.shape, jnp.int32),
        pltpu.SMEM(counts.shape, jnp.int32),
        pltpu.VMEM((3, 2, S, ROWS, 2 * W), F32),
        pltpu.VMEM((3, 2, S, ROWS, 2 * W), F32),
        pltpu.VMEM((2, S, ROWS, 2 * W), F32),
        pltpu.VMEM((2, W, W), F32),
        pltpu.VMEM((2, W, W), F32),
        pltpu.VMEM((2, W, W), F32),
        pltpu.VMEM((len(BITS), W, W), F32),
        pltpu.VMEM((len(BITS), W, W), F32),
        pltpu.VMEM(parts.shape, BF16),
        pltpu.VMEM((4, 2 * W, 4 * W), BF16),
        pltpu.VMEM((4, 6 * W, 2 * W), BF16),
        pltpu.VMEM((ROWS, W), jnp.int32),
        pltpu.VMEM((SCAN, ROWS, W), jnp.int32),
        pltpu.VMEM((SCAN, ROWS, W), jnp.int32),
        pltpu.VMEM((2 + SCAN, ROWS, W), jnp.int32),
        pltpu.VMEM((2 + SCAN, ROWS, W), jnp.int32),
        pltpu.VMEM((ITERS, S, 2, 2, W // 2, W), F32),
        pltpu.VMEM((ITERS, S, SCAN, 2, 2, ROWS, W), F32),
        pltpu.VMEM((ITERS, S, 2, 2, W // 2, W), F32),
        pltpu.VMEM((ITERS, S, SCAN, 2, 2, ROWS, W), F32),
        pltpu.VMEM((ITERS, S, 3, 2, ROWS, 2 * W), F32),
        pltpu.VMEM((S, 6, 2, ROWS, 2 * W), F32),
        pltpu.VMEM((S, 2, 2, ROWS, 2 * W), F32),
        dma((5,)),
    ]
    shapes = {
        "meta_own": (SCAN - 1,),
        "meta_work": (SCAN,),
        "near": (S, 2),
        "meas": (1,),
        "hand": (len(BITS),),
        "replica": (1,),
        "gather": (ITERS, S, SCAN),
        "reduce": (ITERS, S, SCAN),
        "cross": (S, len(CROSS)),
        "base": (1,),
        "last": (S, len(LAST)),
    }
    for shape in shapes.values():
        scratch += [dma(shape), dma(shape)]
    return pl.pallas_call(
        functools.partial(kernel, tiles, tuple(shapes)),
        out_shape=jax.ShapeDtypeStruct(object_slices.shape, F32),
        in_specs=[hbm] * 6,
        out_specs=pl.BlockSpec(memory_space=pltpu.VMEM),
        scratch_shapes=scratch,
        compiler_params=pltpu.CompilerParams(
            collective_id=0, has_side_effects=True, vmem_limit_bytes=VMEM_BYTES
        ),
    )(offsets, counts, object_slices, probe_wave, measured, jnp.asarray(parts))


def solution(mesh):
    placed = (
        P(None, None, ("tile", "scan"), None),
        P(),
        P(("tile", "scan"), None),
        P(("tile", "scan")),
        P(("tile", "scan"), None, None),
    )
    return jax.shard_map(
        functools.partial(body, mesh.shape["tile"]),
        mesh=mesh,
        in_specs=placed,
        out_specs=P(None, None, ("tile", "scan"), None),
        check_vma=False,
    )
```

```python
import functools

import jax
import jax.numpy as jnp
import ml_dtypes
import numpy as np
from jax import lax
from jax.experimental import pallas as pl
from jax.experimental.pallas import tpu as pltpu
from jax.sharding import PartitionSpec as P


ITERS = 2
S = 4
W = 128
SCAN = 8
FAR_FIRST = (2, 6, 1, 3, 5, 7, 4, 0)
ROWS = 8
PROP, PROP_C, DFT, DFT_C = range(4)
MESH = pl.DeviceIdType.MESH
F32 = jnp.float32
BF16 = jnp.bfloat16
VMEM_BYTES = 60 * 2**20


def tables():
    n = np.arange(W)
    dft = np.exp(-2j * np.pi * (n[:, None] * n[None, :] % W) / W) / np.sqrt(W)
    freq = (n + W // 2) % W - W // 2
    prop = np.conj(dft) @ (np.exp(-1j * np.pi * freq * freq / (2.0 * W))[:, None] * dft)
    parts = []
    for part in (prop.real, prop.imag, dft.real, dft.imag):
        high = part.astype(ml_dtypes.bfloat16)
        parts += [high, (part - high.astype(np.float64)).astype(ml_dtypes.bfloat16)]
    return np.stack(parts)


def spread(parts_ref, left_ref, right_ref):
    for which, (first, sign) in enumerate(((0, 1), (0, -1), (4, 1), (4, -1))):
        for place, low in enumerate((0, 0, 1)):
            re = parts_ref[first + low]
            im = parts_ref[first + 2 + low]
            plus, minus = (im, -im) if sign == 1 else (-im, im)
            at = low * 2 * W
            if place:
                left_ref[which, :W, at : at + W] = re
                left_ref[which, :W, at + W : at + 2 * W] = minus
                left_ref[which, W:, at : at + W] = plus
                left_ref[which, W:, at + W : at + 2 * W] = re
            at = place * 2 * W
            right_ref[which, at : at + W, :W] = re
            right_ref[which, at : at + W, W:] = plus
            right_ref[which, at + W : at + 2 * W, :W] = minus
            right_ref[which, at + W : at + 2 * W, W:] = re


def halves(value):
    high = value.astype(BF16)
    return high, (value - high.astype(F32)).astype(BF16)


def sandwich(re, im, left_ref, right_ref, which):
    high, low = halves(jnp.concatenate([re, im], axis=0))
    left = left_ref[which]
    both = jnp.dot(left[:, : 2 * W], jnp.concatenate([high, low], axis=1), preferred_element_type=F32)
    mid = both[:, :W] + both[:, W:] + jnp.dot(left[:, 2 * W :], high, preferred_element_type=F32)
    high, low = halves(jnp.concatenate([mid[:W], mid[W:]], axis=1))
    rows = jnp.concatenate([high, low, high], axis=1)
    right = right_ref[which]
    upper = jnp.dot(rows[: W // 2], right, preferred_element_type=F32)
    lower = jnp.dot(rows[W // 2 :], right, preferred_element_type=F32)
    out = jnp.concatenate([upper, lower], axis=0)
    return out[:, :W], out[:, W:]


def mul(a, b):
    return a[0] * b[0] - a[1] * b[1], a[0] * b[1] + a[1] * b[0]


def mul_conj(a, b):
    return a[0] * b[0] + a[1] * b[1], a[0] * b[1] - a[1] * b[0]


def shifted(value, amount, axis):
    for bit in range(7):
        moved = pltpu.roll(value, 1 << bit, axis)
        value = jnp.where(lax.rem(lax.div(amount, 1 << bit), 2) == 1, moved, value)
    return value

class Links:
    def __init__(self, sems):
        self.sems = sems
        self.started = []
        self.open = {}

    def send(self, name, index, src, dst, device):
        send_sem, recv_sem = self.sems[name]
        copy = pltpu.make_async_remote_copy(
            src_ref=src, dst_ref=dst, send_sem=send_sem.at[index], recv_sem=recv_sem.at[index], device_id=device,
            device_id_type=MESH,
        )
        copy.start()
        self.started.append(copy)
        self.open[name, index] = copy

    def receive(self, name, index, dst=None):
        copy = self.open.pop((name, index))
        if dst is not None:
            copy = pltpu.make_async_remote_copy(
                src_ref=copy.src_ref, dst_ref=dst, send_sem=copy.src_sem, recv_sem=copy.dst_sem,
                device_id=copy.device_id, device_id_type=MESH,
            )
        copy.wait_recv()

    def finish(self):
        for copy in self.started:
            copy.wait_send()


CROSS = ((1, 1, 2, 0), (-1, 0, 2, 2), (2, 2, 1, 4), (-2, 0, 1, 5))
LAST = ((1, 2), (-1, 0))
STAGES = ((4, 4, (1, 2)), (2, 3, (1,)), (1, 1, ()))


def twin(tile, scan):
    core, half, odd = lax.rem(tile, 2), lax.div(scan, 4), lax.rem(lax.div(tile, 2), 2)
    return tile - core + half + 2 - 4 * odd, lax.rem(scan, 4) + 4 * core


def kernel(
    tiles, names, offsets_hbm, counts_hbm, object_hbm, probe_hbm, measured_hbm, parts_hbm, out_ref,
    offsets_ref, counts_ref, obj, obj_work, out_base, probe, shift_probe, meas, meas_out, meas_in, parts, left, right, meta_out,
    meta_own, meta_work, jobs_own, jobs_work, patch, gather_out, grad, grad_in, part, cross_in, last_in, local_sem,
    *sems,
):
    links = Links({name: (sems[2 * i], sems[2 * i + 1]) for i, name in enumerate(names)})
    tile = lax.axis_index("tile")
    me = lax.axis_index("scan")
    region, member = twin(tile, me)

    def ring(first, j):
        return lax.rem(first + j + SCAN, SCAN)

    owners = [(tile, ring(me, j)) for j in range(SCAN)]
    workers = [twin(tile, ring(me, j)) for j in range(SCAN)]
    members = [twin(region, ring(member, j)) for j in range(SCAN)]
    region_owners = [(region, ring(member, j)) for j in range(SCAN)]
    partners = []
    for _, pair, _ in STAGES:
        other = member
        for bit in (1, 2, 4):
            if pair % (2 * bit) // bit:
                other = other + bit - 2 * bit * lax.rem(lax.div(member, bit), 2)
        partners.append(twin(region, other))
    near = {d: (lax.rem(tile + d + tiles, tiles), me) for d in (-1, 1)}
    around = {d: twin(lax.rem(region + d + tiles, tiles), member) for d in (-2, -1, 1, 2)}

    def rows_of(s):
        return pl.ds(pl.multiple_of(s * ROWS, ROWS), ROWS)

    local = {}
    for n, (name, src, dst) in enumerate(
        (
            ("offsets", offsets_hbm, offsets_ref),
            ("counts", counts_hbm, counts_ref),
            ("probe", probe_hbm, probe),
            ("object", object_hbm, obj.at[1]),
            ("parts", parts_hbm, parts),
        )
    ):
        local[name] = pltpu.make_async_copy(src, dst, local_sem.at[n])
        local[name].start()

    barrier = pltpu.get_barrier_semaphore()
    others = owners[1:] + workers + members[1:] + region_owners + list(near.values()) + list(around.values())
    for device in others:
        pl.semaphore_signal(barrier, inc=1, device_id=device, device_id_type=MESH)

    row = lax.broadcasted_iota(jnp.int32, (ROWS, W), 0)
    lane = lax.broadcasted_iota(jnp.int32, (ROWS, W), 1)
    local.pop("offsets").wait()
    local.pop("counts").wait()
    fields = [counts_ref[0], offsets_ref[0, 0], offsets_ref[0, 1], offsets_ref[1, 0], offsets_ref[1, 1]]
    packed = jnp.zeros((ROWS, W), jnp.int32)
    for f, field in enumerate(fields):
        packed = jnp.where(row == f, field, packed)
    meta_out[...] = packed
    meta_own[me] = packed

    pl.semaphore_wait(barrier, len(others))

    for j in range(1, SCAN):
        links.send("meta_own", (j - 1,), meta_out, meta_own.at[me], owners[j])
    for j in range(SCAN):
        links.send("meta_work", (j,), meta_out, meta_work.at[me], workers[j])
    for k in range(S):
        links.send("near", (k, 0), object_hbm.at[:, k], obj.at[0, :, k], near[1])
        links.send("near", (k, 1), object_hbm.at[:, k], obj.at[2, :, k], near[-1])
    links.send("meas", (0,), measured_hbm, meas, workers[0])
    local.pop("probe").wait()
    intensity = probe[0] * probe[0] + probe[1] * probe[1]
    step = 0.5 / (jnp.max(intensity, keepdims=True) + 1e-06)
    local.pop("parts").wait()
    spread(parts, left, right)

    def partner(value, bit):
        if bit == 3:
            return partner(partner(value, 1), 2)
        upper = lax.rem(lax.div(row, bit), 2) == 1
        if bit == SCAN // 2:
            return pltpu.roll(value, bit, 0)
        return jnp.where(upper, pltpu.roll(value, bit, 0), pltpu.roll(value, SCAN - bit, 0))

    def assign(meta, jobs):
        fields = []
        for f in range(5):
            field = jnp.zeros((ROWS, W), jnp.int32)
            for s in range(SCAN):
                field = jnp.where(row == s, meta[s, f : f + 1, :], field)
            fields.append(field)
        count, lower, upper = fields[0], fields[1:3], fields[3:5]
        for n, (bit, pair, rest) in enumerate(STAGES):
            total = count
            for other in rest:
                total = total + partner(total, other)
            excess = total - partner(total, bit)
            eager = jnp.where(count > partner(count, pair), 1, 0)
            rank = jnp.zeros((ROWS, W), jnp.int32)
            ahead = eager
            for other in rest:
                rank = rank + jnp.where(lax.rem(lax.div(row, other), 2) == 1, partner(ahead, other), 0)
                ahead = ahead + partner(ahead, other)
            give = jnp.where((eager == 1) & (2 * rank < excess), 1, 0)
            take = partner(give, pair)
            jobs[2 + n] = count
            jobs[5 + n] = take
            for i in range(2):
                handed = partner(jnp.where(count == 2, upper[i], lower[i]), pair)
                lower[i] = jnp.where((take == 1) & (count == 0), handed, lower[i])
                upper[i] = jnp.where((take == 1) & (count == 1), handed, upper[i])
            count = count + take - give
        jobs[0] = lower[0]
        jobs[1] = lower[1]

    def hand_over(n):
        count = jobs_work[2 + n, pl.ds(member, 1), :]
        meas_out[n] = jnp.where(count == 2, meas[1], meas[0])
        links.send("hand", (n,), meas_out.at[n], meas_in.at[n], partners[n])

    def take_over(n):
        links.receive("hand", (n,))
        count = jobs_work[2 + n, pl.ds(member, 1), :]
        take = jobs_work[5 + n, pl.ds(member, 1), :]
        for i in range(2):
            meas[i] = jnp.where((take == 1) & (count == i), meas_in[n], meas[i])

    def masks(jobs, worker, place):
        wide = jnp.broadcast_to(jobs[1, pl.ds(worker, 1), :], (ROWS, W))
        tall = jnp.broadcast_to(jobs[0, pl.ds(worker, 1), :], (ROWS, W))
        return lane >= wide, place * ROWS + row >= tall

    def gather(it, k):
        jobs, bands_ref, place, targets = (
            (jobs_work, obj_work, member, members) if it else (jobs_own, obj, me, workers)
        )
        bands = [[[bands_ref[b, p, k, :, h * W : (h + 1) * W] for h in range(2)] for p in range(2)] for b in range(3)]
        for j in FAR_FIRST:
            left_part, before = masks(jobs, ring(place, j), place)
            for p in range(2):
                prev, own, after = [jnp.where(left_part, bands[b][p][0], bands[b][p][1]) for b in range(3)]
                merged = jnp.where(before, prev, after)
                if j == 0 and it:
                    patch[it, k, p, 0, rows_of(place), :] = merged
                    patch[it, k, p, 1, rows_of(place), :] = own
                else:
                    gather_out[it, k, j, p, 0] = merged
                    gather_out[it, k, j, p, 1] = own
            if j or not it:
                links.send(
                    "gather", (it, k, j), gather_out.at[it, k, j], patch.at[it, k, :, :, rows_of(place), :], targets[j]
                )

    for j in range(1, SCAN):
        links.receive("meta_own", (j - 1,), meta_own.at[ring(me, -j)])
    assign(meta_own, jobs_own)
    local.pop("object").wait()
    for k in range(S):
        links.receive("near", (k, 0))
        links.receive("near", (k, 1))
        gather(0, k)
        if k == 0:
            for j in range(SCAN):
                links.receive("meta_work", (j,), meta_work.at[ring(member, -j)])
            assign(meta_work, jobs_work)
            links.receive("meas", (0,))
            hand_over(0)
        if k == 1:
            take_over(0)
            hand_over(1)

    take_over(1)
    hand_over(2)
    my_row = jobs_work[0, pl.ds(member, 1), :]
    my_col = jobs_work[1, pl.ds(member, 1), :]
    for p in range(2):
        shift_probe[p] = shifted(shifted(probe[p], my_row, 0), my_col, 1)

    for it in range(ITERS):
        final = it == ITERS - 1

        def fetch(k):
            for j in range(1 if it else 0, SCAN):
                links.receive("gather", (it, k, j), patch.at[it, k, :, :, rows_of(ring(member, -j)), :])
            return patch[it, k, 0].reshape(W, W), patch[it, k, 1].reshape(W, W)

        def reduce_start(k, value):
            for p in range(2):
                grad[it, k, p] = value[p].reshape(2, W // 2, W)
            for j in FAR_FIRST if final else FAR_FIRST[:-1]:
                links.send(
                    "reduce", (it, k, j), grad.at[it, k, :, :, rows_of(ring(member, j)), :], grad_in.at[it, k, j],
                    region_owners[j] if final else members[j],
                )

        def reduce_end(k):
            jobs, place = (jobs_own, me) if final else (jobs_work, member)
            zero = jnp.zeros((ROWS, W), F32)
            total = [[[zero, zero] for p in range(2)] for b in range(3)]
            for j in range(SCAN):
                left_part, before = masks(jobs, ring(place, -j), place)
                if j or final:
                    links.receive("reduce", (it, k, j))
                for p in range(2):
                    if j or final:
                        merged, own = grad_in[it, k, j, p, 0], grad_in[it, k, j, p, 1]
                    else:
                        merged, own = grad[it, k, p, 0, rows_of(place), :], grad[it, k, p, 1, rows_of(place), :]
                    for b, term in ((0, jnp.where(before, merged, 0.0)), (1, own), (2, jnp.where(before, 0.0, merged))):
                        total[b][p][0] = total[b][p][0] + jnp.where(left_part, term, 0.0)
                        total[b][p][1] = total[b][p][1] + jnp.where(left_part, 0.0, term)
            for b in range(3):
                for p in range(2):
                    for h in range(2):
                        part[it, k, b, p, :, h * W : (h + 1) * W] = total[b][p][h]

        def pass_on(k):
            reduce_end(k)
            if final:
                for n, (d, b) in enumerate(LAST):
                    links.send("last", (k, n), part.at[it, k, b], last_in.at[k, n], near[d])
            else:
                for n, (d, b, w, at) in enumerate(CROSS):
                    links.send("cross", (k, n), part.at[it, k, pl.ds(b, w)], cross_in.at[k, pl.ds(at, w)], around[d])

        def update(k):
            if final:
                for n in range(len(LAST)):
                    links.receive("last", (k, n))
                for p in range(2):
                    gradient = part[it, k, 1, p] + last_in[k, 0, p] + last_in[k, 1, p]
                    out_ref[p, k] = out_base[p, k] - step * gradient
            else:
                for n in range(len(CROSS)):
                    links.receive("cross", (k, n))
                for b, (one, two) in enumerate(((0, 4), (1, 2), (3, 5))):
                    for p in range(2):
                        gradient = part[it, k, b, p] + cross_in[k, one, p] + cross_in[k, two, p]
                        obj_work[b, p, k] = obj_work[b, p, k] - step * gradient
                gather(it + 1, k)

        shone = (shift_probe[0], shift_probe[1])
        arrived = [shone]
        patches = [fetch(0)]
        wave = mul(shone, patches[0])
        for k in range(1, S):
            arrived.append(sandwich(*wave, left, right, PROP))
            patches.append(fetch(k))
            if it == 0 and k == 2:
                links.send("replica", (0,), obj, obj_work, workers[0])
            wave = mul(arrived[k], patches[k])
        far = sandwich(*wave, left, right, DFT)
        if it == 0:
            take_over(2)
        ratio = meas[0] * lax.rsqrt(jnp.maximum(far[0] * far[0] + far[1] * far[1], 0.04))
        back = sandwich(far[0] - ratio * far[0], far[1] - ratio * far[1], left, right, DFT_C)
        for k in range(S - 1, 0, -1):
            reduce_start(k, mul_conj(arrived[k], back))
            back = sandwich(*mul_conj(patches[k], back), left, right, PROP_C)
        reduce_start(0, mul_conj(shone, back))

        for k in range(S - 1, 0, -1):
            pass_on(k)
        if not final:
            pass_on(0)
        links.receive("base" if final else "replica", (0,))
        update(3)
        if final:
            pass_on(0)
        update(2)
        update(1)
        update(0)
        if not final:
            links.send("base", (0,), obj_work.at[1], out_base, region_owners[0])

    links.finish()


def body(tiles, object_slices, probe_wave, offsets, counts, measured):
    parts = tables()
    dma = pltpu.SemaphoreType.DMA
    hbm = pl.BlockSpec(memory_space=pltpu.HBM)
    scratch = [
        pltpu.SMEM(offsets.shape, jnp.int32),
        pltpu.SMEM(counts.shape, jnp.int32),
        pltpu.VMEM((3, 2, S, ROWS, 2 * W), F32),
        pltpu.VMEM((3, 2, S, ROWS, 2 * W), F32),
        pltpu.VMEM((2, S, ROWS, 2 * W), F32),
        pltpu.VMEM((2, W, W), F32),
        pltpu.VMEM((2, W, W), F32),
        pltpu.VMEM((2, W, W), F32),
        pltpu.VMEM((len(STAGES), W, W), F32),
        pltpu.VMEM((len(STAGES), W, W), F32),
        pltpu.VMEM(parts.shape, BF16),
        pltpu.VMEM((4, 2 * W, 4 * W), BF16),
        pltpu.VMEM((4, 6 * W, 2 * W), BF16),
        pltpu.VMEM((ROWS, W), jnp.int32),
        pltpu.VMEM((SCAN, ROWS, W), jnp.int32),
        pltpu.VMEM((SCAN, ROWS, W), jnp.int32),
        pltpu.VMEM((2 + SCAN, ROWS, W), jnp.int32),
        pltpu.VMEM((2 + SCAN, ROWS, W), jnp.int32),
        pltpu.VMEM((ITERS, S, 2, 2, W // 2, W), F32),
        pltpu.VMEM((ITERS, S, SCAN, 2, 2, ROWS, W), F32),
        pltpu.VMEM((ITERS, S, 2, 2, W // 2, W), F32),
        pltpu.VMEM((ITERS, S, SCAN, 2, 2, ROWS, W), F32),
        pltpu.VMEM((ITERS, S, 3, 2, ROWS, 2 * W), F32),
        pltpu.VMEM((S, 6, 2, ROWS, 2 * W), F32),
        pltpu.VMEM((S, 2, 2, ROWS, 2 * W), F32),
        dma((5,)),
    ]
    shapes = {
        "meta_own": (SCAN - 1,),
        "meta_work": (SCAN,),
        "near": (S, 2),
        "meas": (1,),
        "hand": (len(STAGES),),
        "replica": (1,),
        "gather": (ITERS, S, SCAN),
        "reduce": (ITERS, S, SCAN),
        "cross": (S, len(CROSS)),
        "base": (1,),
        "last": (S, len(LAST)),
    }
    for shape in shapes.values():
        scratch += [dma(shape), dma(shape)]
    return pl.pallas_call(
        functools.partial(kernel, tiles, tuple(shapes)),
        out_shape=jax.ShapeDtypeStruct(object_slices.shape, F32),
        in_specs=[hbm] * 6,
        out_specs=pl.BlockSpec(memory_space=pltpu.VMEM),
        scratch_shapes=scratch,
        compiler_params=pltpu.CompilerParams(
            collective_id=0, has_side_effects=True, vmem_limit_bytes=VMEM_BYTES
        ),
    )(offsets, counts, object_slices, probe_wave, measured, jnp.asarray(parts))


def solution(mesh):
    placed = (
        P(None, None, ("tile", "scan"), None),
        P(),
        P(("tile", "scan"), None),
        P(("tile", "scan")),
        P(("tile", "scan"), None, None),
    )
    return jax.shard_map(
        functools.partial(body, mesh.shape["tile"]),
        mesh=mesh,
        in_specs=placed,
        out_specs=P(None, None, ("tile", "scan"), None),
        check_vma=False,
    )
```

```python
import functools

import jax
import jax.numpy as jnp
import ml_dtypes
import numpy as np
from jax import lax
from jax.experimental import pallas as pl
from jax.experimental.pallas import tpu as pltpu
from jax.sharding import PartitionSpec as P


ITERS = 2
S = 4
W = 128
SCAN = 8
FAR_FIRST = (2, 6, 1, 3, 5, 7, 4, 0)
ROWS = 8
PROP, PROP_C, DFT, DFT_C = range(4)
MESH = pl.DeviceIdType.MESH
F32 = jnp.float32
BF16 = jnp.bfloat16
VMEM_BYTES = 60 * 2**20


def tables():
    n = np.arange(W)
    dft = np.exp(-2j * np.pi * (n[:, None] * n[None, :] % W) / W) / np.sqrt(W)
    freq = (n + W // 2) % W - W // 2
    prop = np.conj(dft) @ (np.exp(-1j * np.pi * freq * freq / (2.0 * W))[:, None] * dft)
    parts = []
    for part in (prop.real, prop.imag, dft.real, dft.imag):
        high = part.astype(ml_dtypes.bfloat16)
        parts += [high, (part - high.astype(np.float64)).astype(ml_dtypes.bfloat16)]
    return np.stack(parts)


def spread(parts_ref, left_ref, right_ref):
    for which, (first, sign) in enumerate(((0, 1), (0, -1), (4, 1), (4, -1))):
        for place, low in enumerate((0, 0, 1)):
            re = parts_ref[first + low]
            im = parts_ref[first + 2 + low]
            plus, minus = (im, -im) if sign == 1 else (-im, im)
            at = low * 2 * W
            if place:
                left_ref[which, :W, at : at + W] = re
                left_ref[which, :W, at + W : at + 2 * W] = minus
                left_ref[which, W:, at : at + W] = plus
                left_ref[which, W:, at + W : at + 2 * W] = re
            at = place * 2 * W
            right_ref[which, at : at + W, :W] = re
            right_ref[which, at : at + W, W:] = plus
            right_ref[which, at + W : at + 2 * W, :W] = minus
            right_ref[which, at + W : at + 2 * W, W:] = re


def halves(value):
    high = value.astype(BF16)
    return high, (value - high.astype(F32)).astype(BF16)


def sandwich(re, im, left_ref, right_ref, which):
    high, low = halves(jnp.concatenate([re, im], axis=0))
    left = left_ref[which]
    both = jnp.dot(left[:, : 2 * W], jnp.concatenate([high, low], axis=1), preferred_element_type=F32)
    mid = both[:, :W] + both[:, W:] + jnp.dot(left[:, 2 * W :], high, preferred_element_type=F32)
    high, low = halves(jnp.concatenate([mid[:W], mid[W:]], axis=1))
    rows = jnp.concatenate([high, low, high], axis=1)
    right = right_ref[which]
    upper = jnp.dot(rows[: W // 2], right, preferred_element_type=F32)
    lower = jnp.dot(rows[W // 2 :], right, preferred_element_type=F32)
    out = jnp.concatenate([upper, lower], axis=0)
    return out[:, :W], out[:, W:]


def mul(a, b):
    return a[0] * b[0] - a[1] * b[1], a[0] * b[1] + a[1] * b[0]


def mul_conj(a, b):
    return a[0] * b[0] + a[1] * b[1], a[0] * b[1] - a[1] * b[0]


def shifted(value, amount, axis):
    for bit in range(7):
        moved = pltpu.roll(value, 1 << bit, axis)
        value = jnp.where(lax.rem(lax.div(amount, 1 << bit), 2) == 1, moved, value)
    return value

class Links:
    def __init__(self, sems):
        self.sems = sems
        self.started = []
        self.open = {}

    def send(self, name, index, src, dst, device):
        send_sem, recv_sem = self.sems[name]
        copy = pltpu.make_async_remote_copy(
            src_ref=src, dst_ref=dst, send_sem=send_sem.at[index], recv_sem=recv_sem.at[index], device_id=device,
            device_id_type=MESH,
        )
        copy.start()
        self.started.append(copy)
        self.open[name, index] = copy

    def receive(self, name, index, dst=None):
        copy = self.open.pop((name, index))
        if dst is not None:
            copy = pltpu.make_async_remote_copy(
                src_ref=copy.src_ref, dst_ref=dst, send_sem=copy.src_sem, recv_sem=copy.dst_sem,
                device_id=copy.device_id, device_id_type=MESH,
            )
        copy.wait_recv()

    def finish(self):
        for copy in self.started:
            copy.wait_send()


CROSS = ((1, 1, 2, 0), (-1, 0, 2, 2), (2, 2, 1, 4), (-2, 0, 1, 5))
LAST = ((1, 2), (-1, 0))
STAGES = ((4, 4, (1, 2)), (2, 3, (1,)), (1, 1, ()))


def twin(tile, scan):
    core, half, odd = lax.rem(tile, 2), lax.div(scan, 4), lax.rem(lax.div(tile, 2), 2)
    return tile - core + half + 2 - 4 * odd, lax.rem(scan, 4) + 4 * core


def kernel(
    tiles, names, offsets_hbm, counts_hbm, object_hbm, probe_hbm, measured_hbm, parts_hbm, out_ref,
    offsets_ref, counts_ref, obj, obj_work, out_base, probe, shift_probe, meas, meas_out, meas_in, parts, left, right, meta_out,
    meta_own, meta_work, jobs_own, jobs_work, patch, gather_out, grad, grad_in, part, cross_in, last_in, local_sem,
    *sems,
):
    links = Links({name: (sems[2 * i], sems[2 * i + 1]) for i, name in enumerate(names)})
    tile = lax.axis_index("tile")
    me = lax.axis_index("scan")
    region, member = twin(tile, me)

    def ring(first, j):
        return lax.rem(first + j + SCAN, SCAN)

    owners = [(tile, ring(me, j)) for j in range(SCAN)]
    workers = [twin(tile, ring(me, j)) for j in range(SCAN)]
    members = [twin(region, ring(member, j)) for j in range(SCAN)]
    region_owners = [(region, ring(member, j)) for j in range(SCAN)]
    partners = []
    for _, pair, _ in STAGES:
        other = member
        for bit in (1, 2, 4):
            if pair % (2 * bit) // bit:
                other = other + bit - 2 * bit * lax.rem(lax.div(member, bit), 2)
        partners.append(twin(region, other))
    near = {d: (lax.rem(tile + d + tiles, tiles), me) for d in (-1, 1)}
    around = {d: twin(lax.rem(region + d + tiles, tiles), member) for d in (-2, -1, 1, 2)}

    def rows_of(s):
        return pl.ds(pl.multiple_of(s * ROWS, ROWS), ROWS)

    local = {}
    for n, (name, src, dst) in enumerate(
        (
            ("offsets", offsets_hbm, offsets_ref),
            ("counts", counts_hbm, counts_ref),
            ("probe", probe_hbm, probe),
            ("object", object_hbm, obj.at[1]),
            ("parts", parts_hbm, parts),
        )
    ):
        local[name] = pltpu.make_async_copy(src, dst, local_sem.at[n])
        local[name].start()

    barrier = pltpu.get_barrier_semaphore()
    others = owners[1:] + workers + members[1:] + region_owners + list(near.values()) + list(around.values())
    for device in others:
        pl.semaphore_signal(barrier, inc=1, device_id=device, device_id_type=MESH)

    row = lax.broadcasted_iota(jnp.int32, (ROWS, W), 0)
    lane = lax.broadcasted_iota(jnp.int32, (ROWS, W), 1)
    local.pop("offsets").wait()
    local.pop("counts").wait()
    fields = [counts_ref[0], offsets_ref[0, 0], offsets_ref[0, 1], offsets_ref[1, 0], offsets_ref[1, 1]]
    packed = jnp.zeros((ROWS, W), jnp.int32)
    for f, field in enumerate(fields):
        packed = jnp.where(row == f, field, packed)
    meta_out[...] = packed
    meta_own[me] = packed

    pl.semaphore_wait(barrier, len(others))

    for j in FAR_FIRST[:-1]:
        links.send("meta_own", (j - 1,), meta_out, meta_own.at[me], owners[j])
    links.send("near", (0, 0), object_hbm.at[:, 0], obj.at[0, :, 0], near[1])
    links.send("near", (0, 1), object_hbm.at[:, 0], obj.at[2, :, 0], near[-1])
    for j in range(SCAN):
        links.send("meta_work", (j,), meta_out, meta_work.at[me], workers[j])
    for k in range(1, S):
        links.send("near", (k, 0), object_hbm.at[:, k], obj.at[0, :, k], near[1])
        links.send("near", (k, 1), object_hbm.at[:, k], obj.at[2, :, k], near[-1])
    links.send("meas", (0,), measured_hbm, meas, workers[0])
    local.pop("probe").wait()
    intensity = probe[0] * probe[0] + probe[1] * probe[1]
    step = 0.5 / (jnp.max(intensity, keepdims=True) + 1e-06)
    local.pop("parts").wait()
    spread(parts, left, right)

    def partner(value, bit):
        if bit == 3:
            return partner(partner(value, 1), 2)
        upper = lax.rem(lax.div(row, bit), 2) == 1
        if bit == SCAN // 2:
            return pltpu.roll(value, bit, 0)
        return jnp.where(upper, pltpu.roll(value, bit, 0), pltpu.roll(value, SCAN - bit, 0))

    def assign(meta, jobs):
        fields = []
        for f in range(5):
            field = jnp.zeros((ROWS, W), jnp.int32)
            for s in range(SCAN):
                field = jnp.where(row == s, meta[s, f : f + 1, :], field)
            fields.append(field)
        count, lower, upper = fields[0], fields[1:3], fields[3:5]
        for n, (bit, pair, rest) in enumerate(STAGES):
            total = count
            for other in rest:
                total = total + partner(total, other)
            excess = total - partner(total, bit)
            eager = jnp.where(count > partner(count, pair), 1, 0)
            rank = jnp.zeros((ROWS, W), jnp.int32)
            ahead = eager
            for other in rest:
                rank = rank + jnp.where(lax.rem(lax.div(row, other), 2) == 1, partner(ahead, other), 0)
                ahead = ahead + partner(ahead, other)
            give = jnp.where((eager == 1) & (2 * rank < excess), 1, 0)
            take = partner(give, pair)
            jobs[2 + n] = count
            jobs[5 + n] = take
            for i in range(2):
                handed = partner(jnp.where(count == 2, upper[i], lower[i]), pair)
                lower[i] = jnp.where((take == 1) & (count == 0), handed, lower[i])
                upper[i] = jnp.where((take == 1) & (count == 1), handed, upper[i])
            count = count + take - give
        jobs[0] = lower[0]
        jobs[1] = lower[1]

    def hand_over(n):
        count = jobs_work[2 + n, pl.ds(member, 1), :]
        meas_out[n] = jnp.where(count == 2, meas[1], meas[0])
        links.send("hand", (n,), meas_out.at[n], meas_in.at[n], partners[n])

    def take_over(n):
        links.receive("hand", (n,))
        count = jobs_work[2 + n, pl.ds(member, 1), :]
        take = jobs_work[5 + n, pl.ds(member, 1), :]
        for i in range(2):
            meas[i] = jnp.where((take == 1) & (count == i), meas_in[n], meas[i])

    def masks(jobs, worker, place):
        wide = jnp.broadcast_to(jobs[1, pl.ds(worker, 1), :], (ROWS, W))
        tall = jnp.broadcast_to(jobs[0, pl.ds(worker, 1), :], (ROWS, W))
        return lane >= wide, place * ROWS + row >= tall

    def gather(it, k):
        jobs, bands_ref, place, targets = (
            (jobs_work, obj_work, member, members) if it else (jobs_own, obj, me, workers)
        )
        bands = [[[bands_ref[b, p, k, :, h * W : (h + 1) * W] for h in range(2)] for p in range(2)] for b in range(3)]
        for j in FAR_FIRST:
            left_part, before = masks(jobs, ring(place, j), place)
            for p in range(2):
                prev, own, after = [jnp.where(left_part, bands[b][p][0], bands[b][p][1]) for b in range(3)]
                merged = jnp.where(before, prev, after)
                if j == 0 and it:
                    patch[it, k, p, 0, rows_of(place), :] = merged
                    patch[it, k, p, 1, rows_of(place), :] = own
                else:
                    gather_out[it, k, j, p, 0] = merged
                    gather_out[it, k, j, p, 1] = own
            if j or not it:
                links.send(
                    "gather", (it, k, j), gather_out.at[it, k, j], patch.at[it, k, :, :, rows_of(place), :], targets[j]
                )

    for j in range(1, SCAN):
        links.receive("meta_own", (j - 1,), meta_own.at[ring(me, -j)])
    assign(meta_own, jobs_own)
    local.pop("object").wait()
    for k in range(S):
        links.receive("near", (k, 0))
        links.receive("near", (k, 1))
        gather(0, k)
        if k == 0:
            for j in range(SCAN):
                links.receive("meta_work", (j,), meta_work.at[ring(member, -j)])
            assign(meta_work, jobs_work)
            links.receive("meas", (0,))
            hand_over(0)
        if k == 1:
            take_over(0)
            hand_over(1)

    take_over(1)
    hand_over(2)
    my_row = jobs_work[0, pl.ds(member, 1), :]
    my_col = jobs_work[1, pl.ds(member, 1), :]
    for p in range(2):
        shift_probe[p] = shifted(shifted(probe[p], my_row, 0), my_col, 1)

    for it in range(ITERS):
        final = it == ITERS - 1

        def fetch(k):
            for j in range(1 if it else 0, SCAN):
                links.receive("gather", (it, k, j), patch.at[it, k, :, :, rows_of(ring(member, -j)), :])
            return patch[it, k, 0].reshape(W, W), patch[it, k, 1].reshape(W, W)

        def reduce_start(k, value):
            for p in range(2):
                grad[it, k, p] = value[p].reshape(2, W // 2, W)
            for j in FAR_FIRST if final else FAR_FIRST[:-1]:
                links.send(
                    "reduce", (it, k, j), grad.at[it, k, :, :, rows_of(ring(member, j)), :], grad_in.at[it, k, j],
                    region_owners[j] if final else members[j],
                )

        def reduce_end(k):
            jobs, place = (jobs_own, me) if final else (jobs_work, member)
            zero = jnp.zeros((ROWS, W), F32)
            total = [[[zero, zero] for p in range(2)] for b in range(3)]
            for j in range(SCAN):
                left_part, before = masks(jobs, ring(place, -j), place)
                if j or final:
                    links.receive("reduce", (it, k, j))
                for p in range(2):
                    if j or final:
                        merged, own = grad_in[it, k, j, p, 0], grad_in[it, k, j, p, 1]
                    else:
                        merged, own = grad[it, k, p, 0, rows_of(place), :], grad[it, k, p, 1, rows_of(place), :]
                    for b, term in ((0, jnp.where(before, merged, 0.0)), (1, own), (2, jnp.where(before, 0.0, merged))):
                        total[b][p][0] = total[b][p][0] + jnp.where(left_part, term, 0.0)
                        total[b][p][1] = total[b][p][1] + jnp.where(left_part, 0.0, term)
            for b in range(3):
                for p in range(2):
                    for h in range(2):
                        part[it, k, b, p, :, h * W : (h + 1) * W] = total[b][p][h]

        def pass_on(k):
            reduce_end(k)
            if final:
                for n, (d, b) in enumerate(LAST):
                    links.send("last", (k, n), part.at[it, k, b], last_in.at[k, n], near[d])
            else:
                for n, (d, b, w, at) in enumerate(CROSS):
                    links.send("cross", (k, n), part.at[it, k, pl.ds(b, w)], cross_in.at[k, pl.ds(at, w)], around[d])

        def update(k):
            if final:
                for n in range(len(LAST)):
                    links.receive("last", (k, n))
                for p in range(2):
                    gradient = part[it, k, 1, p] + last_in[k, 0, p] + last_in[k, 1, p]
                    out_ref[p, k] = out_base[p, k] - step * gradient
            else:
                for n in range(len(CROSS)):
                    links.receive("cross", (k, n))
                for b, (one, two) in enumerate(((0, 4), (1, 2), (3, 5))):
                    for p in range(2):
                        gradient = part[it, k, b, p] + cross_in[k, one, p] + cross_in[k, two, p]
                        obj_work[b, p, k] = obj_work[b, p, k] - step * gradient
                gather(it + 1, k)

        shone = (shift_probe[0], shift_probe[1])
        arrived = [shone]
        patches = [fetch(0)]
        wave = mul(shone, patches[0])
        for k in range(1, S):
            arrived.append(sandwich(*wave, left, right, PROP))
            patches.append(fetch(k))
            if it == 0 and k == 2:
                links.send("replica", (0,), obj, obj_work, workers[0])
            wave = mul(arrived[k], patches[k])
        far = sandwich(*wave, left, right, DFT)
        if it == 0:
            take_over(2)
        ratio = meas[0] * lax.rsqrt(jnp.maximum(far[0] * far[0] + far[1] * far[1], 0.04))
        back = sandwich(far[0] - ratio * far[0], far[1] - ratio * far[1], left, right, DFT_C)
        for k in range(S - 1, 0, -1):
            reduce_start(k, mul_conj(arrived[k], back))
            back = sandwich(*mul_conj(patches[k], back), left, right, PROP_C)
        reduce_start(0, mul_conj(shone, back))

        for k in range(S - 1, 0, -1):
            pass_on(k)
        if not final:
            pass_on(0)
        links.receive("base" if final else "replica", (0,))
        update(3)
        if final:
            pass_on(0)
        update(2)
        update(1)
        update(0)
        if not final:
            links.send("base", (0,), obj_work.at[1], out_base, region_owners[0])

    links.finish()


def body(tiles, object_slices, probe_wave, offsets, counts, measured):
    parts = tables()
    dma = pltpu.SemaphoreType.DMA
    hbm = pl.BlockSpec(memory_space=pltpu.HBM)
    scratch = [
        pltpu.SMEM(offsets.shape, jnp.int32),
        pltpu.SMEM(counts.shape, jnp.int32),
        pltpu.VMEM((3, 2, S, ROWS, 2 * W), F32),
        pltpu.VMEM((3, 2, S, ROWS, 2 * W), F32),
        pltpu.VMEM((2, S, ROWS, 2 * W), F32),
        pltpu.VMEM((2, W, W), F32),
        pltpu.VMEM((2, W, W), F32),
        pltpu.VMEM((2, W, W), F32),
        pltpu.VMEM((len(STAGES), W, W), F32),
        pltpu.VMEM((len(STAGES), W, W), F32),
        pltpu.VMEM(parts.shape, BF16),
        pltpu.VMEM((4, 2 * W, 4 * W), BF16),
        pltpu.VMEM((4, 6 * W, 2 * W), BF16),
        pltpu.VMEM((ROWS, W), jnp.int32),
        pltpu.VMEM((SCAN, ROWS, W), jnp.int32),
        pltpu.VMEM((SCAN, ROWS, W), jnp.int32),
        pltpu.VMEM((2 + SCAN, ROWS, W), jnp.int32),
        pltpu.VMEM((2 + SCAN, ROWS, W), jnp.int32),
        pltpu.VMEM((ITERS, S, 2, 2, W // 2, W), F32),
        pltpu.VMEM((ITERS, S, SCAN, 2, 2, ROWS, W), F32),
        pltpu.VMEM((ITERS, S, 2, 2, W // 2, W), F32),
        pltpu.VMEM((ITERS, S, SCAN, 2, 2, ROWS, W), F32),
        pltpu.VMEM((ITERS, S, 3, 2, ROWS, 2 * W), F32),
        pltpu.VMEM((S, 6, 2, ROWS, 2 * W), F32),
        pltpu.VMEM((S, 2, 2, ROWS, 2 * W), F32),
        dma((5,)),
    ]
    shapes = {
        "meta_own": (SCAN - 1,),
        "meta_work": (SCAN,),
        "near": (S, 2),
        "meas": (1,),
        "hand": (len(STAGES),),
        "replica": (1,),
        "gather": (ITERS, S, SCAN),
        "reduce": (ITERS, S, SCAN),
        "cross": (S, len(CROSS)),
        "base": (1,),
        "last": (S, len(LAST)),
    }
    for shape in shapes.values():
        scratch += [dma(shape), dma(shape)]
    return pl.pallas_call(
        functools.partial(kernel, tiles, tuple(shapes)),
        out_shape=jax.ShapeDtypeStruct(object_slices.shape, F32),
        in_specs=[hbm] * 6,
        out_specs=pl.BlockSpec(memory_space=pltpu.VMEM),
        scratch_shapes=scratch,
        compiler_params=pltpu.CompilerParams(
            collective_id=0, has_side_effects=True, vmem_limit_bytes=VMEM_BYTES
        ),
    )(offsets, counts, object_slices, probe_wave, measured, jnp.asarray(parts))


def solution(mesh):
    placed = (
        P(None, None, ("tile", "scan"), None),
        P(),
        P(("tile", "scan"), None),
        P(("tile", "scan")),
        P(("tile", "scan"), None, None),
    )
    return jax.shard_map(
        functools.partial(body, mesh.shape["tile"]),
        mesh=mesh,
        in_specs=placed,
        out_specs=P(None, None, ("tile", "scan"), None),
        check_vma=False,
    )
```
